512 devices in a mesh: lat: 16 (over y_lo, x, core), lon: 32 (over y_hi, z).
Axes of the slice: x: 4, y: 8 (y_hi: 4, y_lo: 2; y = y_hi * 2 + y_lo), z: 8, core: 2. Of those that a mesh axis runs over, the one named last changes fastest.
Arguments:
- field: bfloat16 [128, 1024, 256], P('lat', 'lon'), may hold values from -6 to 6
- kernel: float32 [7, 7, 256], replicated, may hold values from -0.875 to 0.875
- gain: float32 [256], replicated, may hold values from 0.1 to 1.9
- w_in: bfloat16 [256, 1024], replicated, may hold values from -0.375 to 0.375
- b_in: float32 [1024], replicated, may hold values from -1 to 1
- w_out: bfloat16 [1024, 256], replicated, may hold values from -0.1875 to 0.1875
- layer_scale: float32 [256], replicated, may hold values from 0.3 to 1.5
- cotangent: bfloat16 [128, 1024, 256], P('lat', 'lon'), may hold values from -6 to 6
Outputs:
- block_out: bfloat16 [128, 1024, 256], P('lat', 'lon')
- grad_field: bfloat16 [128, 1024, 256], P('lat', 'lon')
- grad_kernel: float32 [7, 7, 256], replicated
- grad_gain: float32 [256], replicated
- grad_w_in: float32 [256, 1024], P(None, ('lat', 'lon'))
- grad_b_in: float32 [1024], replicated
- grad_w_out: float32 [1024, 256], P(('lat', 'lon'))
- grad_scale: float32 [256], replicated
The draws below stay inside these ranges and needn't reach their ends.
All inputs are finite; a program needn't handle non-finite values.
Results may differ from the reference program's by a relative error of at most 0.013.
Values may be sent and summed in bfloat16 or wider, within the bound.
A program may use at most 64 MiB of HBM per device.

```python
import math
import jax
import jax.numpy as jnp
from jax import lax

C = 256
FF = 1024
H = 128
W = 1024


def block_scale(key, extent, shards, smallest, largest):
    level, own = 1.0, jax.random.fold_in(key, 6)
    for axis_at, parts in shards:
        steps = jnp.exp(jax.random.uniform(jax.random.fold_in(own, axis_at), (parts,), jnp.float32, smallest / len(shards), largest / len(shards)))
        level = level * jnp.repeat(steps, extent[axis_at] // parts).reshape([-1 if axis == axis_at else 1 for axis in range(len(extent))])
    return level


def noise(key, shape, width, most, split=(), kind=jnp.bfloat16):
    values = width * jax.random.normal(key, shape, jnp.float32)
    if split:
        values = values * block_scale(key, shape, split, -0.22, 0.18)
    return jnp.clip(values, -most, most).astype(kind)


def setup_inputs(seed: int = 0) -> dict:
    splits = jax.random.split(jax.random.key(seed), 9)
    return {
        "field": noise(splits[0], (H, W, C), 1.0, 6.0, ((0, 16), (1, 32))),
        "kernel": noise(splits[1], (7, 7, C), 49 ** -0.5, 0.875, (), jnp.float32),
        "gain": jnp.clip(1.0 + 0.18 * jax.random.normal(splits[2], (C,), jnp.float32), 0.1, 1.9),
        "w_in": noise(splits[3], (C, FF), C ** -0.5, 0.375),
        "b_in": jnp.clip(jax.random.uniform(splits[4], (FF,), jnp.float32, -1.0, 1.0), -1.0, 1.0),
        "w_out": noise(splits[5], (FF, C), FF ** -0.5, 0.1875),
        "layer_scale": jnp.clip(jnp.exp(jax.random.uniform(splits[6], (C,), jnp.float32, math.log(0.3), math.log(1.5))), 0.3, 1.5),
        "cotangent": noise(splits[7], (H, W, C), 1.0, 6.0, ((0, 16), (1, 32))),
    }


GELU_K = 0.7978845608028654
GELU_C = 0.044715
LN_EPSILON = 1e-06

def gelu_pair(pre_act):
    inner = GELU_K * (pre_act + GELU_C * pre_act * pre_act * pre_act)
    tanh_val = jnp.tanh(inner)
    value = 0.5 * pre_act * (1.0 + tanh_val)
    gelu_slope = 0.5 * (1.0 + tanh_val) + 0.5 * pre_act * (1.0 - tanh_val * tanh_val) * GELU_K * (1.0 + 3.0 * GELU_C * pre_act * pre_act)
    return (value, gelu_slope)

def wrap_pad(grid):
    widened = jnp.concatenate([grid[:, -3:], grid, grid[:, :3]], axis=1)
    return jnp.pad(widened, ((3, 3), (0, 0), (0, 0)))

def depthwise(padded, kernel, grid_rows, grid_cols):
    summed = jnp.zeros((grid_rows, grid_cols, kernel.shape[2]), jnp.float32)
    for row_tap in range(7):
        for col_tap in range(7):
            summed = summed + padded[row_tap:row_tap + grid_rows, col_tap:col_tap + grid_cols, :].astype(jnp.float32) * kernel[row_tap, col_tap]
    return summed

def kernel_terms(padded, d_conv, grid_rows, grid_cols):
    taps = []
    for row_tap in range(7):
        for col_tap in range(7):
            window = padded[row_tap:row_tap + grid_rows, col_tap:col_tap + grid_cols, :].astype(jnp.float32)
            taps.append(lax.optimization_barrier(jnp.sum(window * d_conv, axis=(0, 1))))
    return jnp.stack(taps).reshape(7, 7, d_conv.shape[2])

def contract_rows(left, right):
    return lax.dot_general(left, right, (((0,), (0,)), ((), ())), preferred_element_type=jnp.float32)

def pointwise(conv, source, cotangent, gain, w_in, b_in, w_out, layer_scale):
    row_mean = lax.optimization_barrier(jnp.mean(conv, axis=-1, keepdims=True))
    centred = conv - row_mean
    inv_dev = lax.rsqrt(lax.optimization_barrier(jnp.mean(centred * centred, axis=-1, keepdims=True)) + LN_EPSILON)
    normed_hat = centred * inv_dev
    normed = (normed_hat * gain).astype(jnp.bfloat16)
    pre_act = jnp.dot(normed, w_in, preferred_element_type=jnp.float32) + b_in
    activated, gelu_slope = gelu_pair(pre_act)
    hidden = activated.astype(jnp.bfloat16)
    branch = jnp.dot(hidden, w_out, preferred_element_type=jnp.float32)
    block_out = (source.astype(jnp.float32) + layer_scale * branch).astype(jnp.bfloat16)
    cot_wide = cotangent.astype(jnp.float32)
    d_branch = (layer_scale * cot_wide).astype(jnp.bfloat16)
    g_scale = lax.optimization_barrier(jnp.sum(cot_wide * branch, axis=0))
    g_out = contract_rows(hidden, d_branch)
    d_hidden = lax.dot_general(d_branch, w_out, (((1,), (1,)), ((), ())), preferred_element_type=jnp.float32)
    d_pre = d_hidden * gelu_slope
    d_pre_b = d_pre.astype(jnp.bfloat16)
    g_bias = lax.optimization_barrier(jnp.sum(d_pre, axis=0))
    g_in_t = contract_rows(d_pre_b, normed)
    d_normed = lax.dot_general(d_pre_b, w_in, (((1,), (1,)), ((), ())), preferred_element_type=jnp.float32)
    g_gain = lax.optimization_barrier(jnp.sum(d_normed * normed_hat, axis=0))
    scaled = d_normed * gain
    d_conv = inv_dev * (scaled - lax.optimization_barrier(jnp.mean(scaled, axis=-1, keepdims=True)) - normed_hat * lax.optimization_barrier(jnp.mean(scaled * normed_hat, axis=-1, keepdims=True)))
    return (block_out, d_conv, g_in_t, g_out, g_bias, g_gain, g_scale)

def reference(field, kernel, gain, w_in, b_in, w_out, layer_scale, cotangent):
    grid_rows, grid_cols, channels = field.shape
    padded = wrap_pad(field)
    conv = depthwise(padded, kernel, grid_rows, grid_cols)
    step_rows = 8 if grid_rows % 8 == 0 else grid_rows
    blocks = grid_rows // step_rows

    def one_block(carry, index):
        start = (index * step_rows).astype(jnp.int32)
        conv_rows = lax.dynamic_slice_in_dim(conv, start, step_rows, 0).reshape(-1, channels)
        field_rows = lax.dynamic_slice_in_dim(field, start, step_rows, 0).reshape(-1, channels)
        cot_rows = lax.dynamic_slice_in_dim(cotangent, start, step_rows, 0).reshape(-1, channels)
        block_out, d_conv, g_in_t, g_out, g_bias, g_gain, g_scale = pointwise(conv_rows, field_rows, cot_rows, gain, w_in, b_in, w_out, layer_scale)
        carry = (carry[0] + g_in_t, carry[1] + g_out, carry[2] + g_bias, carry[3] + g_gain, carry[4] + g_scale)
        return (carry, (block_out.reshape(step_rows, grid_cols, channels), d_conv.reshape(step_rows, grid_cols, channels)))
    ff_units = w_in.shape[1]
    start_carry = (jnp.zeros((ff_units, channels), jnp.float32), jnp.zeros((ff_units, channels), jnp.float32), jnp.zeros((ff_units,), jnp.float32), jnp.zeros((channels,), jnp.float32), jnp.zeros((channels,), jnp.float32))
    sums, stacked = lax.scan(one_block, start_carry, jnp.arange(blocks, dtype=jnp.int32))
    block_out = stacked[0].reshape(grid_rows, grid_cols, channels)
    d_conv = stacked[1].reshape(grid_rows, grid_cols, channels)
    flipped = kernel[::-1, ::-1, :]
    back = depthwise(wrap_pad(d_conv), flipped, grid_rows, grid_cols)
    grad_field = (cotangent.astype(jnp.float32) + back).astype(jnp.bfloat16)
    factor = 1.0 / jnp.sqrt(jnp.float32(grid_rows * grid_cols))
    grad_kernel = kernel_terms(padded, d_conv, grid_rows, grid_cols) * factor
    grad_w_in = (sums[0] * factor).T
    grad_w_out = sums[1] * factor
    grad_b_in = sums[2] * factor
    grad_gain = sums[3] * factor
    grad_scale = sums[4] * factor
    return (block_out, grad_field, grad_kernel, grad_gain, grad_w_in, grad_b_in, grad_w_out, grad_scale)
```

```python
import jax
import jax.numpy as jnp
from jax import lax
from jax.experimental import pallas as pl
from jax.experimental.pallas import tpu as pltpu
from jax.sharding import PartitionSpec as P

GELU_K = 0.7978845608028654
GELU_C = 0.044715
LN_EPSILON = 1e-06
F32 = jnp.float32
BF16 = jnp.bfloat16
MESH = pl.DeviceIdType.MESH

N_X, N_Y, N_Z = 4, 8, 8
N_LAT, N_LON = 16, 32
ROWS, COLS, CH, FF = 8, 32, 256, 1024
CELLS = ROWS * COLS
HALF = 128
LEFT = 8
CHUNKS = 4
CHUNK = FF // CHUNKS
SUMS = 64
FACTOR = 1.0 / 131072.0**0.5


def dot(left, right, over_left, over_right):
    return lax.dot_general(
        left, right, (((over_left,), (over_right,)), ((), ())), preferred_element_type=F32
    )


class Place:
    def __init__(self):
        self.lat = lax.axis_index("lat")
        self.lon = lax.axis_index("lon")
        self.core = lax.rem(self.lat, 2)
        self.x = lax.rem(self.lat // 2, N_X)
        self.y_lo = self.lat // 8
        self.z = lax.rem(self.lon, N_Z)
        self.y_hi = self.lon // N_Z
        self.y = self.y_hi * 2 + self.y_lo

    def grid(self, down, right):
        return (
            lax.rem(self.lat + down + N_LAT, N_LAT),
            lax.rem(self.lon + right + N_LON, N_LON),
        )

    def sibling(self):
        return (self.lat + 1 - 2 * self.core, self.lon)

    def on_x(self, x):
        return (self.y_lo * 8 + x * 2 + self.core, self.lon)

    def on_y(self, y):
        return (lax.rem(y, 2) * 8 + self.x * 2 + self.core, (y // 2) * N_Z + self.z)

    def on_z(self, z):
        return (self.lat, self.y_hi * N_Z + z)


def remote(src, dst, send, recv, device):
    return pltpu.make_async_remote_copy(
        src_ref=src, dst_ref=dst, send_sem=send, recv_sem=recv, device_id=device, device_id_type=MESH
    )


SIDES = ((-1, 0), (1, 0), (0, -1), (0, 1), (-1, -1), (-1, 1), (1, -1), (1, 1))


def halo_pack(pad, tmp, rows_out, cols_out):
    for half in range(2):
        lanes = slice(half * HALF, (half + 1) * HALF)
        rows_out[0, :, :, lanes] = pad[half, 3:6, LEFT : LEFT + COLS, :].astype(BF16)
        rows_out[1, :, :, lanes] = pad[half, 8:11, LEFT : LEFT + COLS, :].astype(BF16)
        for row in range(ROWS):
            tmp[0, row * 4 : row * 4 + 4, lanes] = pad[half, 3 + row, LEFT : LEFT + 4, :]
            tmp[1, row * 4 : row * 4 + 4, lanes] = pad[half, 3 + row, LEFT + 28 : LEFT + 32, :]
    cols_out[...] = tmp[...].astype(BF16)


def halo_copies(place, rows_out, cols_out, rows_in, cols_in, corners_in, send, recv):
    pairs = (
        (rows_out.at[0], rows_in.at[1]),
        (rows_out.at[1], rows_in.at[0]),
        (cols_out.at[0], cols_in.at[1]),
        (cols_out.at[1], cols_in.at[0]),
        (cols_out.at[0, 0:16], corners_in.at[3]),
        (cols_out.at[1, 0:16], corners_in.at[2]),
        (cols_out.at[0, 16:32], corners_in.at[1]),
        (cols_out.at[1, 16:32], corners_in.at[0]),
    )
    return [
        remote(src, dst, send.at[at], recv.at[at], place.grid(*SIDES[at]))
        for at, (src, dst) in enumerate(pairs)
    ]


def halo_unpack(place, pad, rows_in, cols_in, corners_in):
    above = jnp.where(place.lat == 0, 0.0, 1.0).astype(F32)
    below = jnp.where(place.lat == N_LAT - 1, 0.0, 1.0).astype(F32)
    for half in range(2):
        lanes = slice(half * HALF, (half + 1) * HALF)
        pad[half, 0:3, LEFT : LEFT + COLS, :] = rows_in[0, :, :, lanes].astype(F32) * above
        pad[half, 11:14, LEFT : LEFT + COLS, :] = rows_in[1, :, :, lanes].astype(F32) * below
        for side, at in ((0, LEFT - 4), (1, LEFT + COLS)):
            wide = cols_in[side, :, lanes].astype(F32)
            for row in range(ROWS):
                pad[half, 3 + row, at : at + 4, :] = wide[row * 4 : row * 4 + 4]
            top = corners_in[side, :, lanes].astype(F32) * above
            bottom = corners_in[2 + side, :, lanes].astype(F32) * below
            for row in range(3):
                pad[half, row, at : at + 4, :] = top[4 + row * 4 : 8 + row * 4]
                pad[half, 11 + row, at : at + 4, :] = bottom[row * 4 : row * 4 + 4]


def depthwise(pad, taps, out, flipped):
    def one_half(half, carry):
        lanes = pl.ds(pl.multiple_of(half * HALF, HALF), HALF)
        for col in range(0, COLS, 8):
            summed = jnp.zeros((ROWS, 8, HALF), F32)
            for b in range(7):
                start = LEFT - 3 + b + col
                window = pad[half, :, start : start + 8, :]
                for a in range(7):
                    at = (6 - a, 6 - b) if flipped else (a, b)
                    tap = taps[at[0], at[1] : at[1] + 1, lanes]
                    summed = summed + window[a : a + ROWS] * tap[None]
            out[half, :, col : col + 8, :] = summed
        return carry

    lax.fori_loop(0, 2, one_half, 0)


def tap_sums(pad, d_pad, sums):
    def one_half(half, carry):
        lanes = pl.ds(pl.multiple_of(half * HALF, HALF), HALF)
        for b in range(7):
            totals = [jnp.zeros((8, HALF), F32) for _ in range(7)]
            for col in range(0, COLS, 8):
                start = LEFT - 3 + b + col
                window = pad[half, :, start : start + 8, :]
                grads = d_pad[half, 3 : 3 + ROWS, LEFT + col : LEFT + col + 8, :]
                for a in range(7):
                    totals[a] = totals[a] + jnp.sum(window[a : a + ROWS] * grads, axis=0)
            for a in range(7):
                at = a * 7 + b
                sums[at : at + 1, lanes] = jnp.sum(totals[a], axis=0, keepdims=True)
        return carry

    lax.fori_loop(0, 2, one_half, 0)


def gelu_pair(pre_act):
    square = pre_act * pre_act
    tanh_val = jnp.tanh(GELU_K * pre_act * (1.0 + GELU_C * square))
    half_up = 0.5 + 0.5 * tanh_val
    value = pre_act * half_up
    gelu_slope = half_up + value * (1.0 - tanh_val) * (GELU_K + (3.0 * GELU_C * GELU_K) * square)
    return value, gelu_slope


def step(
    field, taps, gain, w_in, b_in, w_out, layer_scale, cotangent,
    block_out, grad_field, small_out, large_out,
    pad, d_pad, conv, hat, normed, d_branch, inv_all, tmp,
    rows_out, cols_out, rows_in, cols_in, corners_in,
    d_rows_out, d_cols_out, d_rows_in, d_cols_in, d_corners_in,
    part, part_in, x_out, x_in, y_out, y_in, z_out, z_in,
    sums, sums_out, sums_in, sx, sy_a, sz_b, sz_a, sy_b, s_final,
    halo_send, halo_recv, d_halo_send, d_halo_recv,
    core_send, core_recv, x_send, x_recv, y_send, y_recv, z_send, z_recv,
    s_core_send, s_core_recv, sx_send, sx_recv, s3_send, s3_recv, s4_send, s4_recv, s_all_send, s_all_recv,
):
    place = Place()
    core, x, y, z = place.core, place.x, place.y, place.z

    barrier = pltpu.get_barrier_semaphore()
    partners = [place.grid(*side) for side in SIDES]
    partners.append(place.sibling())
    partners += [place.on_x(lax.rem(x + k, N_X)) for k in range(1, N_X)]
    partners += [place.on_y(lax.rem(y + k, N_Y)) for k in range(1, N_Y)]
    partners += [place.on_z(lax.rem(z + k, N_Z)) for k in range(1, N_Z)]
    for device in partners:
        pl.semaphore_signal(barrier, inc=1, device_id=device, device_id_type=MESH)

    for half in range(2):
        lanes = slice(half * HALF, (half + 1) * HALF)
        pad[half, 3 : 3 + ROWS, LEFT : LEFT + COLS, :] = field[:, :, lanes].astype(F32)
    halo_pack(pad, tmp, rows_out, cols_out)
    wide_cot = cotangent[...].reshape(CELLS, CH).astype(F32)
    d_branch[...] = (layer_scale[...] * wide_cot).astype(BF16)

    pl.semaphore_wait(barrier, len(partners))
    halos = halo_copies(place, rows_out, cols_out, rows_in, cols_in, corners_in, halo_send, halo_recv)
    for copy in halos:
        copy.start()
    for copy in halos:
        copy.wait()
    halo_unpack(place, pad, rows_in, cols_in, corners_in)

    depthwise(pad, taps, conv, False)
    parts = [conv[half].reshape(CELLS, HALF) for half in range(2)]
    mean = jnp.sum(parts[0] + parts[1], axis=-1, keepdims=True) * (1.0 / CH)
    parts = [value - mean for value in parts]
    spread = jnp.sum(parts[0] * parts[0] + parts[1] * parts[1], axis=-1, keepdims=True) * (1.0 / CH)
    inv_dev = lax.rsqrt(spread + LN_EPSILON)
    inv_all[...] = jnp.broadcast_to(inv_dev, (CELLS, HALF))
    for half in range(2):
        lanes = slice(half * HALF, (half + 1) * HALF)
        value = parts[half] * inv_dev
        hat[half] = value
        normed[:, lanes] = (value * gain[:, lanes]).astype(BF16)

    branch = jnp.zeros((CELLS, CH), F32)
    d_normed = jnp.zeros((CELLS, CH), F32)
    core_copies = []
    for chunk in range(CHUNKS):
        hidden_units = slice(chunk * CHUNK, (chunk + 1) * CHUNK)
        pre_act = dot(normed[...], w_in[:, hidden_units], 1, 0) + b_in[:, hidden_units]
        value, gelu_slope = gelu_pair(pre_act)
        hidden = value.astype(BF16)
        d_pre = dot(d_branch[...], w_out[hidden_units, :], 1, 1) * gelu_slope
        d_pre_b = d_pre.astype(BF16)
        part[1, chunk] = dot(hidden, d_branch[...], 0, 0).astype(BF16).reshape(2, 2, 64, CH)
        part[0, chunk] = dot(d_pre_b, normed[...], 0, 0).astype(BF16).reshape(2, 2, 64, CH)
        for which in (1, 0):
            copy = remote(
                part.at[which, chunk, :, 1 - core], part_in.at[which, chunk],
                core_send.at[which, chunk], core_recv.at[which, chunk], place.sibling(),
            )
            copy.start()
            core_copies.append((which, chunk, copy))
        branch = branch + dot(hidden, w_out[hidden_units, :], 1, 0)
        d_normed = d_normed + dot(d_pre_b, w_in[:, hidden_units], 1, 1)
        sums[51 + chunk : 52 + chunk, :] = jnp.sum(d_pre, axis=0, keepdims=True)

    wide_cot = cotangent[...].reshape(CELLS, CH).astype(F32)
    sums[50:51, :] = jnp.sum(wide_cot * branch, axis=0, keepdims=True)
    sums[55:64, :] = jnp.zeros((9, CH), F32)
    block_out[...] = (
        field[...].reshape(CELLS, CH).astype(F32) + layer_scale[...] * branch
    ).astype(BF16).reshape(ROWS, COLS, CH)

    hats = [hat[half] for half in range(2)]
    d_halves = [d_normed[:, half * HALF : (half + 1) * HALF] for half in range(2)]
    scaled = []
    for half in range(2):
        lanes = slice(half * HALF, (half + 1) * HALF)
        sums[49:50, lanes] = jnp.sum(d_halves[half] * hats[half], axis=0, keepdims=True)
        scaled.append(d_halves[half] * gain[:, lanes])
    m1 = jnp.sum(scaled[0] + scaled[1], axis=-1, keepdims=True) * (1.0 / CH)
    m2 = jnp.sum(scaled[0] * hats[0] + scaled[1] * hats[1], axis=-1, keepdims=True) * (1.0 / CH)
    for half in range(2):
        d_conv = inv_all[...] * (scaled[half] - m1 - hats[half] * m2)
        d_pad[half, 3 : 3 + ROWS, LEFT : LEFT + COLS, :] = d_conv.reshape(ROWS, COLS, HALF)

    halo_pack(d_pad, tmp, d_rows_out, d_cols_out)
    d_halos = halo_copies(
        place, d_rows_out, d_cols_out, d_rows_in, d_cols_in, d_corners_in, d_halo_send, d_halo_recv
    )
    for copy in d_halos:
        copy.start()

    x_copies = []
    for which, chunk, copy in core_copies:
        copy.wait()
        both = part[which, chunk, :, core].astype(F32) + part_in[which, chunk].astype(F32)
        x_out[which, chunk // 2, (chunk % 2) * 2 : (chunk % 2) * 2 + 2] = both.astype(BF16)
    for which in (1, 0):
        for k in range(1, N_X):
            to = lax.rem(x + k, N_X)
            copy = remote(
                x_out.at[which, :, to], x_in.at[which, k - 1],
                x_send.at[which, k - 1], x_recv.at[which, k - 1], place.on_x(to),
            )
            copy.start()
            x_copies.append(copy)

    tap_sums(pad, d_pad, sums)

    sums_out[...] = sums[...].reshape(2, SUMS // 2, CH).astype(BF16)
    s_core = remote(sums_out.at[1 - core], sums_in, s_core_send, s_core_recv, place.sibling())
    s_core.start()

    y_copies = []
    for which in (1, 0):
        total = x_out[which, :, x].astype(F32)
        for k in range(1, N_X):
            x_copies[(1 - which) * (N_X - 1) + k - 1].wait()
            total = total + x_in[which, k - 1].astype(F32)
        y_out[which] = total.astype(BF16).reshape(2, 4, 16, CH)
        if which == 1:
            s_core.wait()
            sx[x] = (sums_out[core].astype(F32) + sums_in[...].astype(F32)).astype(BF16)
            sx_copies = []
            for k in range(1, N_X):
                to = lax.rem(x + k, N_X)
                copy = remote(sx.at[x], sx.at[x], sx_send.at[to], sx_recv.at[x], place.on_x(to))
                copy.start()
                sx_copies.append(copy)
        for k in range(1, N_Y):
            to = lax.rem(y + k, N_Y)
            copy = remote(
                y_out.at[which, lax.rem(to, 2), to // 2], y_in.at[which, k - 1],
                y_send.at[which, k - 1], y_recv.at[which, k - 1], place.on_y(to),
            )
            copy.start()
            y_copies.append(copy)

    def gather_sum(slots, count):
        total = slots[0].astype(F32)
        for at in range(1, count):
            total = total + slots[at].astype(F32)
        return total

    def wait_slots(slots, send, recv, own, count, device_on):
        for k in range(1, count):
            other = lax.rem(own + k, count)
            remote(slots.at[own], slots.at[other], send.at[other], recv.at[other], device_on(other)).wait()

    def share(slots, send, recv, own, count, device_on):
        for k in range(1, count):
            other = lax.rem(own + k, count)
            remote(slots.at[own], slots.at[own], send.at[other], recv.at[own], device_on(other)).start()

    wait_slots(sx, sx_send, sx_recv, x, N_X, place.on_x)
    total = gather_sum(sx, N_X).astype(BF16)
    sy_a[y] = total[0:16]
    sz_b[z] = total[16:32]
    share(sy_a, s3_send.at[0], s3_recv.at[0], y, N_Y, place.on_y)
    share(sz_b, s3_send.at[1], s3_recv.at[1], z, N_Z, place.on_z)

    for copy in d_halos:
        copy.wait()
    halo_unpack(place, d_pad, d_rows_in, d_cols_in, d_corners_in)
    depthwise(d_pad, taps, conv, True)
    for half in range(2):
        lanes = slice(half * HALF, (half + 1) * HALF)
        grad_field[:, :, lanes] = (cotangent[:, :, lanes].astype(F32) + conv[half]).astype(BF16)

    for which in (1, 0):
        total = y_out[which, place.y_lo, place.y_hi].astype(F32)
        for k in range(1, N_Y):
            y_copies[(1 - which) * (N_Y - 1) + k - 1].wait()
            total = total + y_in[which, k - 1].astype(F32)
        for to in range(N_Z):
            for half in range(2):
                at = which * 4 + half * 2
                z_out[to, at : at + 2, :] = total[2 * to : 2 * to + 2, half * HALF : (half + 1) * HALF]
    z_copies = []
    for k in range(1, N_Z):
        to = lax.rem(z + k, N_Z)
        copy = remote(z_out.at[to], z_in.at[k - 1], z_send.at[k - 1], z_recv.at[k - 1], place.on_z(to))
        copy.start()
        z_copies.append(copy)

    wait_slots(sy_a, s3_send.at[0], s3_recv.at[0], y, N_Y, place.on_y)
    wait_slots(sz_b, s3_send.at[1], s3_recv.at[1], z, N_Z, place.on_z)
    sz_a[z] = gather_sum(sy_a, N_Y).astype(BF16)
    sy_b[y] = gather_sum(sz_b, N_Z).astype(BF16)
    share(sz_a, s4_send.at[0], s4_recv.at[0], z, N_Z, place.on_z)
    share(sy_b, s4_send.at[1], s4_recv.at[1], y, N_Y, place.on_y)

    total = z_out[z]
    for k in range(1, N_Z):
        z_copies[k - 1].wait()
        total = total + z_in[k - 1]
    large_out[...] = total * FACTOR

    wait_slots(sz_a, s4_send.at[0], s4_recv.at[0], z, N_Z, place.on_z)
    wait_slots(sy_b, s4_send.at[1], s4_recv.at[1], y, N_Y, place.on_y)
    s_final[core, 0:16] = gather_sum(sz_a, N_Z) * FACTOR
    s_final[core, 16:32] = gather_sum(sy_b, N_Y) * FACTOR
    s_all = remote(s_final.at[core], s_final.at[core], s_all_send, s_all_recv, place.sibling())
    s_all.start()
    s_all.wait_send()
    remote(s_final.at[core], s_final.at[1 - core], s_all_send, s_all_recv, place.sibling()).wait_recv()
    small_out[...] = s_final[...].reshape(SUMS, CH)


def finish(
    block_in, field_in, small, large,
    block_out, grad_field, grad_taps, grad_gain, grad_in, grad_bias, grad_out, grad_scale,
):
    block_out[...] = block_in[...]
    grad_field[...] = field_in[...]
    for a in range(7):
        grad_taps[a] = small[a * 7 : a * 7 + 7, :]
    grad_gain[...] = small[49:50, :]
    grad_scale[...] = small[50:51, :]
    for chunk in range(CHUNKS):
        grad_bias[:, chunk * CHUNK : (chunk + 1) * CHUNK] = small[51 + chunk : 52 + chunk, :]
    for half in range(2):
        lanes = slice(half * HALF, (half + 1) * HALF)
        grad_in[:, lanes] = large[half * 2 : half * 2 + 2, :]
        grad_out[:, lanes] = large[4 + half * 2 : 6 + half * 2, :]


def local(field, kernel, gain, w_in, b_in, w_out, layer_scale, cotangent):
    vmem = pl.BlockSpec(memory_space=pltpu.VMEM)
    dma = pltpu.SemaphoreType.DMA
    halo = [
        pltpu.VMEM((2, 3, COLS, CH), BF16),
        pltpu.VMEM((2, 4 * ROWS, CH), BF16),
        pltpu.VMEM((2, 3, COLS, CH), BF16),
        pltpu.VMEM((2, 4 * ROWS, CH), BF16),
        pltpu.VMEM((4, 16, CH), BF16),
    ]
    scratch = [
        pltpu.VMEM((2, ROWS + 6, COLS + 16, HALF), F32),
        pltpu.VMEM((2, ROWS + 6, COLS + 16, HALF), F32),
        pltpu.VMEM((2, ROWS, COLS, HALF), F32),
        pltpu.VMEM((2, CELLS, HALF), F32),
        pltpu.VMEM((CELLS, CH), BF16),
        pltpu.VMEM((CELLS, CH), BF16),
        pltpu.VMEM((CELLS, HALF), F32),
        pltpu.VMEM((2, 4 * ROWS, CH), F32),
        *halo,
        *halo,
        pltpu.VMEM((2, CHUNKS, 2, 2, 64, CH), BF16),
        pltpu.VMEM((2, CHUNKS, 2, 64, CH), BF16),
        pltpu.VMEM((2, 2, N_X, 64, CH), BF16),
        pltpu.VMEM((2, N_X - 1, 2, 64, CH), BF16),
        pltpu.VMEM((2, 2, 4, 16, CH), BF16),
        pltpu.VMEM((2, N_Y - 1, 16, CH), BF16),
        pltpu.VMEM((N_Z, 8, HALF), F32),
        pltpu.VMEM((N_Z - 1, 8, HALF), F32),
        pltpu.VMEM((SUMS, CH), F32),
        pltpu.VMEM((2, SUMS // 2, CH), BF16),
        pltpu.VMEM((SUMS // 2, CH), BF16),
        pltpu.VMEM((N_X, SUMS // 2, CH), BF16),
        pltpu.VMEM((N_Y, 16, CH), BF16),
        pltpu.VMEM((N_Z, 16, CH), BF16),
        pltpu.VMEM((N_Z, 16, CH), BF16),
        pltpu.VMEM((N_Y, 16, CH), BF16),
        pltpu.VMEM((2, SUMS // 2, CH), F32),
        dma((8,)), dma((8,)), dma((8,)), dma((8,)),
        dma((2, CHUNKS)), dma((2, CHUNKS)),
        dma((2, N_X - 1)), dma((2, N_X - 1)),
        dma((2, N_Y - 1)), dma((2, N_Y - 1)),
        dma((N_Z - 1,)), dma((N_Z - 1,)),
        dma, dma,
        dma((N_X,)), dma((N_X,)),
        dma((2, 8)), dma((2, 8)), dma((2, 8)), dma((2, 8)),
        dma, dma,
    ]
    grid_shape = jax.ShapeDtypeStruct(field.shape, BF16)
    mids = pl.pallas_call(
        step,
        out_shape=(
            grid_shape,
            grid_shape,
            jax.ShapeDtypeStruct((SUMS, CH), F32),
            jax.ShapeDtypeStruct((8, HALF), F32),
        ),
        in_specs=[vmem] * 8,
        out_specs=[vmem] * 4,
        scratch_shapes=scratch,
        compiler_params=pltpu.CompilerParams(
            collective_id=0, has_side_effects=True, vmem_limit_bytes=48 * 2**20
        ),
        name="block_step",
    )(
        field, kernel, gain.reshape(1, CH), w_in, b_in.reshape(1, FF), w_out,
        layer_scale.reshape(1, CH), cotangent,
    )
    block_out, grad_field, g_kernel, g_gain, g_in, g_bias, g_out, g_scale = pl.pallas_call(
        finish,
        out_shape=(
            grid_shape,
            grid_shape,
            jax.ShapeDtypeStruct((7, 7, CH), F32),
            jax.ShapeDtypeStruct((1, CH), F32),
            jax.ShapeDtypeStruct((2, CH), F32),
            jax.ShapeDtypeStruct((1, FF), F32),
            jax.ShapeDtypeStruct((2, CH), F32),
            jax.ShapeDtypeStruct((1, CH), F32),
        ),
        in_specs=[vmem] * 4,
        out_specs=[vmem] * 8,
        name="write_outputs",
    )(*mids)
    return (
        block_out,
        grad_field,
        g_kernel,
        g_gain.reshape(CH),
        g_in.T,
        g_bias.reshape(FF),
        g_out,
        g_scale.reshape(CH),
    )


def solution(mesh):
    in_specs = (P("lat", "lon", None), P(), P(), P(), P(), P(), P(), P("lat", "lon", None))
    out_specs = (
        P("lat", "lon", None),
        P("lat", "lon", None),
        P(),
        P(),
        P(None, ("lat", "lon")),
        P(),
        P(("lat", "lon"), None),
        P(),
    )
    return jax.shard_map(local, mesh=mesh, in_specs=in_specs, out_specs=out_specs, check_vma=False)
```

```python
import jax
import jax.numpy as jnp
from jax import lax
from jax.experimental import pallas as pl
from jax.experimental.pallas import tpu as pltpu
from jax.sharding import PartitionSpec as P

GELU_K = 0.7978845608028654
GELU_C = 0.044715
LN_EPSILON = 1e-06
F32 = jnp.float32
BF16 = jnp.bfloat16
MESH = pl.DeviceIdType.MESH

N_X, N_Y, N_Z = 4, 8, 8
N_LAT, N_LON = 16, 32
ROWS, COLS, CH, FF = 8, 32, 256, 1024
CELLS = ROWS * COLS
HALF = 128
LEFT = 8
CHUNKS = 4
CHUNK = FF // CHUNKS
SUMS = 64
VMEM_GRANT = 62 * 2**20
FACTOR = 1.0 / 131072.0**0.5


def dot(left, right, over_left, over_right):
    return lax.dot_general(
        left, right, (((over_left,), (over_right,)), ((), ())), preferred_element_type=F32
    )


class Place:
    def __init__(self):
        self.lat = lax.axis_index("lat")
        self.lon = lax.axis_index("lon")
        self.core = lax.rem(self.lat, 2)
        self.x = lax.rem(self.lat // 2, N_X)
        self.y_lo = self.lat // 8
        self.z = lax.rem(self.lon, N_Z)
        self.y_hi = self.lon // N_Z
        self.y = self.y_hi * 2 + self.y_lo

    def grid(self, down, right):
        return (
            lax.rem(self.lat + down + N_LAT, N_LAT),
            lax.rem(self.lon + right + N_LON, N_LON),
        )

    def sibling(self):
        return (self.lat + 1 - 2 * self.core, self.lon)

    def on_x(self, x, core=None):
        return (self.y_lo * 8 + x * 2 + (self.core if core is None else core), self.lon)

    def on_y(self, y):
        return (lax.rem(y, 2) * 8 + self.x * 2 + self.core, (y // 2) * N_Z + self.z)

    def on_z(self, z):
        return (self.lat, self.y_hi * N_Z + z)


def remote(src, dst, send, recv, device):
    return pltpu.make_async_remote_copy(
        src_ref=src, dst_ref=dst, send_sem=send, recv_sem=recv, device_id=device, device_id_type=MESH
    )


SIDES = ((-1, 0), (1, 0), (0, -1), (0, 1), (-1, -1), (-1, 1), (1, -1), (1, 1))


def halo_pack(pad, tmp, rows_out, cols_out):
    for half in range(2):
        lanes = slice(half * HALF, (half + 1) * HALF)
        rows_out[0, :, :, lanes] = pad[half, 3:6, LEFT : LEFT + COLS, :].astype(BF16)
        rows_out[1, :, :, lanes] = pad[half, 8:11, LEFT : LEFT + COLS, :].astype(BF16)
        for row in range(ROWS):
            tmp[0, row * 4 : row * 4 + 4, lanes] = pad[half, 3 + row, LEFT : LEFT + 4, :]
            tmp[1, row * 4 : row * 4 + 4, lanes] = pad[half, 3 + row, LEFT + 28 : LEFT + 32, :]
    cols_out[...] = tmp[...].astype(BF16)


def halo_copies(place, rows_out, cols_out, rows_in, cols_in, corners_in, send, recv):
    pairs = (
        (rows_out.at[0], rows_in.at[1]),
        (rows_out.at[1], rows_in.at[0]),
        (cols_out.at[0], cols_in.at[1]),
        (cols_out.at[1], cols_in.at[0]),
        (cols_out.at[0, 0:16], corners_in.at[3]),
        (cols_out.at[1, 0:16], corners_in.at[2]),
        (cols_out.at[0, 16:32], corners_in.at[1]),
        (cols_out.at[1, 16:32], corners_in.at[0]),
    )
    return [
        remote(src, dst, send.at[at], recv.at[at], place.grid(*SIDES[at]))
        for at, (src, dst) in enumerate(pairs)
    ]


def halo_unpack(place, pad, rows_in, cols_in, corners_in):
    above = jnp.where(place.lat == 0, 0.0, 1.0).astype(F32)
    below = jnp.where(place.lat == N_LAT - 1, 0.0, 1.0).astype(F32)
    for half in range(2):
        lanes = slice(half * HALF, (half + 1) * HALF)
        pad[half, 0:3, LEFT : LEFT + COLS, :] = rows_in[0, :, :, lanes].astype(F32) * above
        pad[half, 11:14, LEFT : LEFT + COLS, :] = rows_in[1, :, :, lanes].astype(F32) * below
        for side, at in ((0, LEFT - 4), (1, LEFT + COLS)):
            wide = cols_in[side, :, lanes].astype(F32)
            for row in range(ROWS):
                pad[half, 3 + row, at : at + 4, :] = wide[row * 4 : row * 4 + 4]
            top = corners_in[side, :, lanes].astype(F32) * above
            bottom = corners_in[2 + side, :, lanes].astype(F32) * below
            for row in range(3):
                pad[half, row, at : at + 4, :] = top[4 + row * 4 : 8 + row * 4]
                pad[half, 11 + row, at : at + 4, :] = bottom[row * 4 : row * 4 + 4]


def depthwise(pad, taps, out, flipped):
    def one_half(half, carry):
        lanes = pl.ds(pl.multiple_of(half * HALF, HALF), HALF)
        for col in range(0, COLS, 8):
            summed = jnp.zeros((ROWS, 8, HALF), F32)
            for b in range(7):
                start = LEFT - 3 + b + col
                window = pad[half, :, start : start + 8, :]
                for a in range(7):
                    at = (6 - a, 6 - b) if flipped else (a, b)
                    tap = taps[at[0], at[1] : at[1] + 1, lanes]
                    summed = summed + window[a : a + ROWS] * tap[None]
            out[half, :, col : col + 8, :] = summed
        return carry

    lax.fori_loop(0, 2, one_half, 0)


def tap_sums(pad, d_pad, sums):
    def one_half(half, carry):
        lanes = pl.ds(pl.multiple_of(half * HALF, HALF), HALF)
        for b in range(7):
            totals = [jnp.zeros((8, HALF), F32) for _ in range(7)]
            for col in range(0, COLS, 8):
                start = LEFT - 3 + b + col
                window = pad[half, :, start : start + 8, :]
                grads = d_pad[half, 3 : 3 + ROWS, LEFT + col : LEFT + col + 8, :]
                for a in range(7):
                    totals[a] = totals[a] + jnp.sum(window[a : a + ROWS] * grads, axis=0)
            for a in range(7):
                at = a * 7 + b
                sums[at : at + 1, lanes] = jnp.sum(totals[a], axis=0, keepdims=True)
        return carry

    lax.fori_loop(0, 2, one_half, 0)


def gelu_pair(pre_act):
    square = pre_act * pre_act
    tanh_val = jnp.tanh(GELU_K * pre_act * (1.0 + GELU_C * square))
    half_up = 0.5 + 0.5 * tanh_val
    value = pre_act * half_up
    gelu_slope = half_up + value * (1.0 - tanh_val) * (GELU_K + (3.0 * GELU_C * GELU_K) * square)
    return value, gelu_slope


def step(
    field_hbm, taps_hbm, gain_hbm, w_in_hbm, b_in_hbm, w_out_hbm, layer_scale_hbm, cotangent_hbm,
    block_hbm, grad_hbm, small_out, large_out,
    block_out, grad_field, store,
    field, taps, gain, w_in, b_in, w_out, layer_scale, cotangent, load,
    pad, d_pad, conv, hat, normed, d_branch, inv_all, tmp, d_hidden, slope, branch,
    rows_out, cols_out, rows_in, cols_in, corners_in,
    d_rows_out, d_cols_out, d_rows_in, d_cols_in, d_corners_in,
    part, part_in, x_out, x_in, y_out, y_in, z_out, z_in, zy_tmp, zy_out, zy_in, yz_out, yz_in,
    sums, sums_out, sums_in, sx, sy_a, sz_b, sz_a, sy_b,
    halo_send, halo_recv, d_halo_send, d_halo_recv,
    core_send, core_recv, x_send, x_recv, y_send, y_recv, z_send, z_recv,
    zy_send, zy_recv, yz_send, yz_recv,
    s_core_send, s_core_recv, sx_send, sx_recv, s3_send, s3_recv, s4_send, s4_recv,
):
    loads = [
        pltpu.make_async_copy(src, dst, load.at[at])
        for at, (src, dst) in enumerate((
            (field_hbm, field),
            (cotangent_hbm, cotangent),
            (layer_scale_hbm, layer_scale),
            (taps_hbm, taps),
            (gain_hbm, gain),
            (w_in_hbm, w_in),
            (b_in_hbm, b_in),
            (w_out_hbm, w_out),
        ))
    ]
    for copy in loads:
        copy.start()

    place = Place()
    core, x, y, z = place.core, place.x, place.y, place.z

    barrier = pltpu.get_barrier_semaphore()
    partners = [place.grid(*side) for side in SIDES]
    partners.append(place.sibling())
    partners += [place.on_x(lax.rem(x + k, N_X), c) for k in range(1, N_X) for c in range(2)]
    partners += [place.on_y(lax.rem(y + k, N_Y)) for k in range(1, N_Y)]
    partners += [place.on_z(lax.rem(z + k, N_Z)) for k in range(1, N_Z)]
    for device in partners:
        pl.semaphore_signal(barrier, inc=1, device_id=device, device_id_type=MESH)

    loads[0].wait()
    for half in range(2):
        lanes = slice(half * HALF, (half + 1) * HALF)
        pad[half, 3 : 3 + ROWS, LEFT : LEFT + COLS, :] = field[:, :, lanes].astype(F32)
    halo_pack(pad, tmp, rows_out, cols_out)
    pl.semaphore_wait(barrier, len(partners))
    halos = halo_copies(place, rows_out, cols_out, rows_in, cols_in, corners_in, halo_send, halo_recv)
    for copy in halos:
        copy.start()

    for copy in loads[1:]:
        copy.wait()
    wide_cot = cotangent[...].reshape(CELLS, CH).astype(F32)
    d_branch[...] = (layer_scale[...] * wide_cot).astype(BF16)
    for chunk in range(CHUNKS):
        d_hidden[chunk] = dot(d_branch[...], w_out[chunk * CHUNK : (chunk + 1) * CHUNK, :], 1, 1)
    z_out[...] = jnp.zeros_like(z_out)
    yz_out[...] = jnp.zeros_like(yz_out)
    sums[55:64, :] = jnp.zeros((9, CH), F32)

    for copy in halos:
        copy.wait()
    halo_unpack(place, pad, rows_in, cols_in, corners_in)

    depthwise(pad, taps, conv, False)
    parts = [conv[half].reshape(CELLS, HALF) for half in range(2)]
    mean = jnp.sum(parts[0] + parts[1], axis=-1, keepdims=True) * (1.0 / CH)
    parts = [value - mean for value in parts]
    spread = jnp.sum(parts[0] * parts[0] + parts[1] * parts[1], axis=-1, keepdims=True) * (1.0 / CH)
    inv_dev = lax.rsqrt(spread + LN_EPSILON)
    inv_all[...] = jnp.broadcast_to(inv_dev, (CELLS, HALF))
    for half in range(2):
        lanes = slice(half * HALF, (half + 1) * HALF)
        value = parts[half] * inv_dev
        hat[half] = value
        normed[:, lanes] = (value * gain[:, lanes]).astype(BF16)

    core_copies = {}
    x_copies = {}

    def send_on_core(which, chunk, value):
        part[which, chunk] = value.astype(BF16).reshape(2, 2, 64, CH)
        copy = remote(
            part.at[which, chunk, :, 1 - core], part_in.at[which, chunk],
            core_send.at[which, chunk], core_recv.at[which, chunk], place.sibling(),
        )
        copy.start()
        core_copies[which, chunk] = copy

    def send_on_x(which, chunk):
        core_copies[which, chunk].wait()
        both = part[which, chunk, :, core].astype(F32) + part_in[which, chunk].astype(F32)
        row = chunk // 2
        x_out[which, row, (chunk % 2) * 2 : (chunk % 2) * 2 + 2] = both.astype(BF16)
        if chunk % 2 == 1:
            for k in range(1, N_X):
                to = lax.rem(x + k, N_X)
                copy = remote(
                    x_out.at[which, row, to], x_in.at[which, k - 1, row],
                    x_send.at[which, k - 1, row], x_recv.at[which, k - 1, row], place.on_x(to),
                )
                copy.start()
                x_copies[which, k, row] = copy

    total = jnp.zeros((CELLS, CH), F32)
    for chunk in range(CHUNKS):
        hidden_units = slice(chunk * CHUNK, (chunk + 1) * CHUNK)
        pre_act = dot(normed[...], w_in[:, hidden_units], 1, 0) + b_in[:, hidden_units]
        value, gelu_slope = gelu_pair(pre_act)
        hidden = value.astype(BF16)
        slope[chunk] = gelu_slope
        send_on_core(1, chunk, dot(hidden, d_branch[...], 0, 0))
        total = total + dot(hidden, w_out[hidden_units, :], 1, 0)
        if chunk >= 2:
            send_on_x(1, chunk - 2)
    branch[...] = total

    d_normed = jnp.zeros((CELLS, CH), F32)
    for chunk in range(CHUNKS):
        hidden_units = slice(chunk * CHUNK, (chunk + 1) * CHUNK)
        d_pre = d_hidden[chunk] * slope[chunk]
        d_pre_b = d_pre.astype(BF16)
        send_on_core(0, chunk, dot(d_pre_b, normed[...], 0, 0))
        d_normed = d_normed + dot(d_pre_b, w_in[:, hidden_units], 1, 1)
        sums[51 + chunk : 52 + chunk, :] = jnp.sum(d_pre, axis=0, keepdims=True)
        if chunk < 2:
            send_on_x(1, chunk + 2)
        else:
            send_on_x(0, chunk - 2)

    wide_cot = cotangent[...].reshape(CELLS, CH).astype(F32)
    sums[50:51, :] = jnp.sum(wide_cot * branch[...], axis=0, keepdims=True)

    hats = [hat[half] for half in range(2)]
    d_halves = [d_normed[:, half * HALF : (half + 1) * HALF] for half in range(2)]
    scaled = []
    for half in range(2):
        lanes = slice(half * HALF, (half + 1) * HALF)
        sums[49:50, lanes] = jnp.sum(d_halves[half] * hats[half], axis=0, keepdims=True)
        scaled.append(d_halves[half] * gain[:, lanes])
    m1 = jnp.sum(scaled[0] + scaled[1], axis=-1, keepdims=True) * (1.0 / CH)
    m2 = jnp.sum(scaled[0] * hats[0] + scaled[1] * hats[1], axis=-1, keepdims=True) * (1.0 / CH)
    for half in range(2):
        d_conv = inv_all[...] * (scaled[half] - m1 - hats[half] * m2)
        d_pad[half, 3 : 3 + ROWS, LEFT : LEFT + COLS, :] = d_conv.reshape(ROWS, COLS, HALF)

    halo_pack(d_pad, tmp, d_rows_out, d_cols_out)
    d_halos = halo_copies(
        place, d_rows_out, d_cols_out, d_rows_in, d_cols_in, d_corners_in, d_halo_send, d_halo_recv
    )
    for copy in d_halos:
        copy.start()

    send_on_x(0, 2)
    send_on_x(0, 3)

    tap_sums(pad, d_pad, sums)

    def wait_slots(slots, send, recv, own, count, device_on):
        for k in range(1, count):
            other = lax.rem(own + k, count)
            remote(slots.at[own], slots.at[other], send.at[other], recv.at[other], device_on(other)).wait()

    def share(slots, send, recv, own, count, device_on):
        for k in range(1, count):
            other = lax.rem(own + k, count)
            remote(slots.at[own], slots.at[own], send.at[other], recv.at[own], device_on(other)).start()

    def gather_sum(slots, count):
        total = slots[0].astype(F32)
        for at in range(1, count):
            total = total + slots[at].astype(F32)
        return total

    sums_out[...] = sums[...].reshape(2, SUMS // 2, CH).astype(BF16)
    s_core = remote(sums_out.at[1 - core], sums_in, s_core_send, s_core_recv, place.sibling())
    s_core.start()
    s_core.wait()
    total = (sums_out[core].astype(F32) + sums_in[...].astype(F32)).astype(BF16)
    sy_a[y] = total[0:16]
    sz_b[z] = total[16:32]
    share(sy_a, s3_send.at[0], s3_recv.at[0], y, N_Y, place.on_y)
    share(sz_b, s3_send.at[1], s3_recv.at[1], z, N_Z, place.on_z)

    block_out[...] = (
        field[...].reshape(CELLS, CH).astype(F32) + layer_scale[...] * branch[...]
    ).astype(BF16).reshape(ROWS, COLS, CH)
    block_store = pltpu.make_async_copy(block_out, block_hbm, store.at[0])
    block_store.start()
    for copy in d_halos:
        copy.wait()
    halo_unpack(place, d_pad, d_rows_in, d_cols_in, d_corners_in)
    depthwise(d_pad, taps, conv, True)
    for half in range(2):
        lanes = slice(half * HALF, (half + 1) * HALF)
        grad_field[:, :, lanes] = (cotangent[:, :, lanes].astype(F32) + conv[half]).astype(BF16)
    grad_store = pltpu.make_async_copy(grad_field, grad_hbm, store.at[1])
    grad_store.start()

    wait_slots(sy_a, s3_send.at[0], s3_recv.at[0], y, N_Y, place.on_y)
    sz_a[z] = gather_sum(sy_a, N_Y).astype(BF16)
    share(sz_a, s4_send.at[0], s4_recv.at[0], z, N_Z, place.on_z)
    wait_slots(sz_b, s3_send.at[1], s3_recv.at[1], z, N_Z, place.on_z)
    sy_b[y] = gather_sum(sz_b, N_Z).astype(BF16)
    share(sy_b, s4_send.at[1], s4_recv.at[1], y, N_Y, place.on_y)

    def sum_on_x(which):
        for k in range(1, N_X):
            for row in range(2):
                x_copies[which, k, row].wait()
        total = x_out[which, :, x].astype(F32)
        for k in range(1, N_X):
            total = total + x_in[which, k - 1].astype(F32)
        return total

    def spread(into, send, recv, own, count, device_on, block):
        copies = []
        for k in range(1, count):
            to = lax.rem(own + k, count)
            copy = remote(block(to), into.at[k - 1], send.at[k - 1], recv.at[k - 1], device_on(to))
            copy.start()
            copies.append(copy)
        return copies

    def collect(copies, total, into):
        for copy in copies:
            copy.wait()
        for at in range(len(copies)):
            total = total + into[at].astype(F32)
        return total

    y_out[...] = sum_on_x(1).astype(BF16).reshape(2, 4, 16, CH)
    y_copies = spread(
        y_in, y_send, y_recv, y, N_Y, place.on_y,
        lambda to: y_out.at[lax.rem(to, 2), to // 2],
    )
    total = sum_on_x(0).reshape(2, 4, 16, CH)
    for on_y in range(N_Y):
        for on_z in range(N_Z):
            zy_tmp[on_z, 2 * on_y : 2 * on_y + 2, :] = total[on_y % 2, on_y // 2, 2 * on_z : 2 * on_z + 2]
    zy_out[...] = zy_tmp[...].astype(BF16)
    zy_copies = spread(
        zy_in, zy_send, zy_recv, z, N_Z, place.on_z, lambda to: zy_out.at[to]
    )

    wait_slots(sz_a, s4_send.at[0], s4_recv.at[0], z, N_Z, place.on_z)
    wait_slots(sy_b, s4_send.at[1], s4_recv.at[1], y, N_Y, place.on_y)
    sx[core, x, 0:16] = gather_sum(sz_a, N_Z).astype(BF16)
    sx[core, x, 16:32] = gather_sum(sy_b, N_Y).astype(BF16)
    last = [(c, k) for c in range(2) for k in range(N_X) if (c, k) != (0, 0)]
    for c, k in last:
        c, k = lax.rem(core + c, 2), lax.rem(x + k, N_X)
        remote(
            sx.at[core, x], sx.at[core, x], sx_send.at[c, k], sx_recv.at[core, x], place.on_x(k, c)
        ).start()

    def pack(out, first, total):
        for to in range(8):
            for half in range(2):
                at = first + half * 2
                out[to, at : at + 2, :] = total[2 * to : 2 * to + 2, half * HALF : (half + 1) * HALF]

    pack(z_out, 4, collect(y_copies, y_out[place.y_lo, place.y_hi].astype(F32), y_in))
    z_copies = spread(z_in, z_send, z_recv, z, N_Z, place.on_z, lambda to: z_out.at[to])
    pack(yz_out, 0, collect(zy_copies, zy_out[z].astype(F32), zy_in))
    yz_copies = spread(yz_in, yz_send, yz_recv, y, N_Y, place.on_y, lambda to: yz_out.at[to])

    for c, k in last:
        c, k = lax.rem(core + c, 2), lax.rem(x + k, N_X)
        remote(
            sx.at[core, x], sx.at[c, k], sx_send.at[c, k], sx_recv.at[c, k], place.on_x(k, c)
        ).wait()
    for c in range(2):
        small_out[c * (SUMS // 2) : (c + 1) * (SUMS // 2), :] = gather_sum(sx.at[c], N_X) * FACTOR

    large_out[4:8, :] = collect(z_copies, z_out[z], z_in)[4:8] * FACTOR
    large_out[0:4, :] = collect(yz_copies, yz_out[y], yz_in)[0:4] * FACTOR
    block_store.wait()
    grad_store.wait()


def finish(
    block_in, grad_in_hbm, small_hbm, large_hbm,
    block_out, grad_field, grad_taps, grad_gain, grad_in, grad_bias, grad_out, grad_scale,
    small, large, move,
):
    moves = [
        pltpu.make_async_copy(src, dst, move.at[at])
        for at, (src, dst) in enumerate((
            (small_hbm, small), (large_hbm, large), (block_in, block_out), (grad_in_hbm, grad_field),
        ))
    ]
    for copy in moves:
        copy.start()
    moves[0].wait()
    moves[1].wait()
    for a in range(7):
        grad_taps[a] = small[a * 7 : a * 7 + 7, :]
    grad_gain[...] = small[49:50, :]
    grad_scale[...] = small[50:51, :]
    for chunk in range(CHUNKS):
        grad_bias[:, chunk * CHUNK : (chunk + 1) * CHUNK] = small[51 + chunk : 52 + chunk, :]
    for half in range(2):
        lanes = slice(half * HALF, (half + 1) * HALF)
        grad_in[:, lanes] = large[half * 2 : half * 2 + 2, :]
        grad_out[:, lanes] = large[4 + half * 2 : 6 + half * 2, :]
    moves[2].wait()
    moves[3].wait()


def local(field, kernel, gain, w_in, b_in, w_out, layer_scale, cotangent):
    vmem = pl.BlockSpec(memory_space=pltpu.VMEM)
    dma = pltpu.SemaphoreType.DMA
    halo = [
        pltpu.VMEM((2, 3, COLS, CH), BF16),
        pltpu.VMEM((2, 4 * ROWS, CH), BF16),
        pltpu.VMEM((2, 3, COLS, CH), BF16),
        pltpu.VMEM((2, 4 * ROWS, CH), BF16),
        pltpu.VMEM((4, 16, CH), BF16),
    ]
    hbm = pl.BlockSpec(memory_space=pltpu.HBM)
    scratch = [
        pltpu.VMEM((ROWS, COLS, CH), BF16),
        pltpu.VMEM((ROWS, COLS, CH), BF16),
        dma((2,)),
        pltpu.VMEM((ROWS, COLS, CH), BF16),
        pltpu.VMEM((7, 7, CH), F32),
        pltpu.VMEM((1, CH), F32),
        pltpu.VMEM((CH, FF), BF16),
        pltpu.VMEM((1, FF), F32),
        pltpu.VMEM((FF, CH), BF16),
        pltpu.VMEM((1, CH), F32),
        pltpu.VMEM((ROWS, COLS, CH), BF16),
        dma((8,)),
        pltpu.VMEM((2, ROWS + 6, COLS + 16, HALF), F32),
        pltpu.VMEM((2, ROWS + 6, COLS + 16, HALF), F32),
        pltpu.VMEM((2, ROWS, COLS, HALF), F32),
        pltpu.VMEM((2, CELLS, HALF), F32),
        pltpu.VMEM((CELLS, CH), BF16),
        pltpu.VMEM((CELLS, CH), BF16),
        pltpu.VMEM((CELLS, HALF), F32),
        pltpu.VMEM((2, 4 * ROWS, CH), F32),
        pltpu.VMEM((CHUNKS, CELLS, CHUNK), F32),
        pltpu.VMEM((CHUNKS, CELLS, CHUNK), F32),
        pltpu.VMEM((CELLS, CH), F32),
        *halo,
        *halo,
        pltpu.VMEM((2, CHUNKS, 2, 2, 64, CH), BF16),
        pltpu.VMEM((2, CHUNKS, 2, 64, CH), BF16),
        pltpu.VMEM((2, 2, N_X, 64, CH), BF16),
        pltpu.VMEM((2, N_X - 1, 2, 64, CH), BF16),
        pltpu.VMEM((2, 4, 16, CH), BF16),
        pltpu.VMEM((N_Y - 1, 16, CH), BF16),
        pltpu.VMEM((N_Z, 8, HALF), F32),
        pltpu.VMEM((N_Z - 1, 8, HALF), F32),
        pltpu.VMEM((N_Z, 16, CH), F32),
        pltpu.VMEM((N_Z, 16, CH), BF16),
        pltpu.VMEM((N_Z - 1, 16, CH), BF16),
        pltpu.VMEM((N_Y, 8, HALF), F32),
        pltpu.VMEM((N_Y - 1, 8, HALF), F32),
        pltpu.VMEM((SUMS, CH), F32),
        pltpu.VMEM((2, SUMS // 2, CH), BF16),
        pltpu.VMEM((SUMS // 2, CH), BF16),
        pltpu.VMEM((2, N_X, SUMS // 2, CH), BF16),
        pltpu.VMEM((N_Y, 16, CH), BF16),
        pltpu.VMEM((N_Z, 16, CH), BF16),
        pltpu.VMEM((N_Z, 16, CH), BF16),
        pltpu.VMEM((N_Y, 16, CH), BF16),
        dma((8,)), dma((8,)), dma((8,)), dma((8,)),
        dma((2, CHUNKS)), dma((2, CHUNKS)),
        dma((2, N_X - 1, 2)), dma((2, N_X - 1, 2)),
        dma((N_Y - 1,)), dma((N_Y - 1,)), dma((N_Z - 1,)), dma((N_Z - 1,)),
        dma((N_Z - 1,)), dma((N_Z - 1,)), dma((N_Y - 1,)), dma((N_Y - 1,)),
        dma, dma,
        dma((2, N_X)), dma((2, N_X)),
        dma((2, 8)), dma((2, 8)), dma((2, 8)), dma((2, 8)),
    ]
    grid_shape = jax.ShapeDtypeStruct(field.shape, BF16)
    mids = pl.pallas_call(
        step,
        out_shape=(
            grid_shape,
            grid_shape,
            jax.ShapeDtypeStruct((SUMS, CH), F32),
            jax.ShapeDtypeStruct((8, HALF), F32),
        ),
        in_specs=[hbm] * 8,
        out_specs=[hbm, hbm, vmem, vmem],
        scratch_shapes=scratch,
        compiler_params=pltpu.CompilerParams(
            collective_id=0, has_side_effects=True, vmem_limit_bytes=VMEM_GRANT
        ),
        name="block_step",
    )(
        field, kernel, gain.reshape(1, CH), w_in, b_in.reshape(1, FF), w_out,
        layer_scale.reshape(1, CH), cotangent,
    )
    block_out, grad_field, g_kernel, g_gain, g_in, g_bias, g_out, g_scale = pl.pallas_call(
        finish,
        out_shape=(
            grid_shape,
            grid_shape,
            jax.ShapeDtypeStruct((7, 7, CH), F32),
            jax.ShapeDtypeStruct((1, CH), F32),
            jax.ShapeDtypeStruct((2, CH), F32),
            jax.ShapeDtypeStruct((1, FF), F32),
            jax.ShapeDtypeStruct((2, CH), F32),
            jax.ShapeDtypeStruct((1, CH), F32),
        ),
        in_specs=[hbm] * 4,
        out_specs=[vmem] * 8,
        scratch_shapes=[pltpu.VMEM((SUMS, CH), F32), pltpu.VMEM((8, HALF), F32), dma((4,))],
        compiler_params=pltpu.CompilerParams(vmem_limit_bytes=VMEM_GRANT),
        name="write_outputs",
    )(*mids)
    return (
        block_out,
        grad_field,
        g_kernel,
        g_gain.reshape(CH),
        g_in.T,
        g_bias.reshape(FF),
        g_out,
        g_scale.reshape(CH),
    )


def solution(mesh):
    in_specs = (P("lat", "lon", None), P(), P(), P(), P(), P(), P(), P("lat", "lon", None))
    out_specs = (
        P("lat", "lon", None),
        P("lat", "lon", None),
        P(),
        P(),
        P(None, ("lat", "lon")),
        P(),
        P(("lat", "lon"), None),
        P(),
    )
    return jax.shard_map(local, mesh=mesh, in_specs=in_specs, out_specs=out_specs, check_vma=False)
```

```python
import jax
import jax.numpy as jnp
from jax import lax
from jax.experimental import pallas as pl
from jax.experimental.pallas import tpu as pltpu
from jax.sharding import PartitionSpec as P

GELU_K = 0.7978845608028654
GELU_C = 0.044715
LN_EPSILON = 1e-06
F32 = jnp.float32
BF16 = jnp.bfloat16
MESH = pl.DeviceIdType.MESH

N_X, N_Y, N_Z = 4, 8, 8
N_LAT, N_LON = 16, 32
ROWS, COLS, CH, FF = 8, 32, 256, 1024
CELLS = ROWS * COLS
HALF = 128
LEFT = 8
CHUNKS = 4
CHUNK = FF // CHUNKS
SUMS = 64
VMEM_GRANT = 62 * 2**20
FACTOR = 1.0 / 131072.0**0.5


def dot(left, right, over_left, over_right):
    return lax.dot_general(
        left, right, (((over_left,), (over_right,)), ((), ())), preferred_element_type=F32
    )


class Place:
    def __init__(self):
        self.lat = lax.axis_index("lat")
        self.lon = lax.axis_index("lon")
        self.core = lax.rem(self.lat, 2)
        self.x = lax.rem(self.lat // 2, N_X)
        self.y_lo = self.lat // 8
        self.z = lax.rem(self.lon, N_Z)
        self.y_hi = self.lon // N_Z
        self.y = self.y_hi * 2 + self.y_lo

    def grid(self, down, right):
        return (
            lax.rem(self.lat + down + N_LAT, N_LAT),
            lax.rem(self.lon + right + N_LON, N_LON),
        )

    def sibling(self):
        return (self.lat + 1 - 2 * self.core, self.lon)

    def on_x(self, x, core=None):
        return (self.y_lo * 8 + x * 2 + (self.core if core is None else core), self.lon)

    def on_y(self, y):
        return (lax.rem(y, 2) * 8 + self.x * 2 + self.core, (y // 2) * N_Z + self.z)

    def on_z(self, z):
        return (self.lat, self.y_hi * N_Z + z)


def remote(src, dst, send, recv, device):
    return pltpu.make_async_remote_copy(
        src_ref=src, dst_ref=dst, send_sem=send, recv_sem=recv, device_id=device, device_id_type=MESH
    )


SIDES = ((-1, 0), (1, 0), (0, -1), (0, 1), (-1, -1), (-1, 1), (1, -1), (1, 1))


def halo_pack(pad, tmp, rows_out, cols_out):
    for half in range(2):
        lanes = slice(half * HALF, (half + 1) * HALF)
        rows_out[0, :, :, lanes] = pad[half, 3:6, LEFT : LEFT + COLS, :].astype(BF16)
        rows_out[1, :, :, lanes] = pad[half, 8:11, LEFT : LEFT + COLS, :].astype(BF16)
        for row in range(ROWS):
            tmp[0, row * 4 : row * 4 + 4, lanes] = pad[half, 3 + row, LEFT : LEFT + 4, :]
            tmp[1, row * 4 : row * 4 + 4, lanes] = pad[half, 3 + row, LEFT + 28 : LEFT + 32, :]
    cols_out[...] = tmp[...].astype(BF16)


def halo_copies(place, rows_out, cols_out, rows_in, cols_in, corners_in, send, recv):
    pairs = (
        (rows_out.at[0], rows_in.at[1]),
        (rows_out.at[1], rows_in.at[0]),
        (cols_out.at[0], cols_in.at[1]),
        (cols_out.at[1], cols_in.at[0]),
        (cols_out.at[0, 0:16], corners_in.at[3]),
        (cols_out.at[1, 0:16], corners_in.at[2]),
        (cols_out.at[0, 16:32], corners_in.at[1]),
        (cols_out.at[1, 16:32], corners_in.at[0]),
    )
    return [
        remote(src, dst, send.at[at], recv.at[at], place.grid(*SIDES[at]))
        for at, (src, dst) in enumerate(pairs)
    ]


def halo_unpack(place, pad, rows_in, cols_in, corners_in):
    above = jnp.where(place.lat == 0, 0.0, 1.0).astype(F32)
    below = jnp.where(place.lat == N_LAT - 1, 0.0, 1.0).astype(F32)
    for half in range(2):
        lanes = slice(half * HALF, (half + 1) * HALF)
        pad[half, 0:3, LEFT : LEFT + COLS, :] = rows_in[0, :, :, lanes].astype(F32) * above
        pad[half, 11:14, LEFT : LEFT + COLS, :] = rows_in[1, :, :, lanes].astype(F32) * below
        for side, at in ((0, LEFT - 4), (1, LEFT + COLS)):
            wide = cols_in[side, :, lanes].astype(F32)
            for row in range(ROWS):
                pad[half, 3 + row, at : at + 4, :] = wide[row * 4 : row * 4 + 4]
            top = corners_in[side, :, lanes].astype(F32) * above
            bottom = corners_in[2 + side, :, lanes].astype(F32) * below
            for row in range(3):
                pad[half, row, at : at + 4, :] = top[4 + row * 4 : 8 + row * 4]
                pad[half, 11 + row, at : at + 4, :] = bottom[row * 4 : row * 4 + 4]


def depthwise(pad, taps, out, flipped):
    def one_half(half, carry):
        lanes = pl.ds(pl.multiple_of(half * HALF, HALF), HALF)
        for col in range(0, COLS, 8):
            summed = jnp.zeros((ROWS, 8, HALF), F32)
            for b in range(7):
                start = LEFT - 3 + b + col
                window = pad[half, :, start : start + 8, :]
                for a in range(7):
                    at = (6 - a, 6 - b) if flipped else (a, b)
                    tap = taps[at[0], at[1] : at[1] + 1, lanes]
                    summed = summed + window[a : a + ROWS] * tap[None]
            out[half, :, col : col + 8, :] = summed
        return carry

    lax.fori_loop(0, 2, one_half, 0)


def tap_sums(pad, d_pad, sums):
    def one_half(half, carry):
        lanes = pl.ds(pl.multiple_of(half * HALF, HALF), HALF)
        for b in range(7):
            totals = [jnp.zeros((8, HALF), F32) for _ in range(7)]
            for col in range(0, COLS, 8):
                start = LEFT - 3 + b + col
                window = pad[half, :, start : start + 8, :]
                grads = d_pad[half, 3 : 3 + ROWS, LEFT + col : LEFT + col + 8, :]
                for a in range(7):
                    totals[a] = totals[a] + jnp.sum(window[a : a + ROWS] * grads, axis=0)
            for a in range(7):
                at = a * 7 + b
                sums[at : at + 1, lanes] = jnp.sum(totals[a], axis=0, keepdims=True)
        return carry

    lax.fori_loop(0, 2, one_half, 0)


def gelu_pair(pre_act):
    square = pre_act * pre_act
    tanh_val = jnp.tanh(GELU_K * pre_act * (1.0 + GELU_C * square))
    half_up = 0.5 + 0.5 * tanh_val
    value = pre_act * half_up
    gelu_slope = half_up + value * (1.0 - tanh_val) * (GELU_K + (3.0 * GELU_C * GELU_K) * square)
    return value, gelu_slope


def step(
    field_hbm, taps_hbm, gain_hbm, w_in_hbm, b_in_hbm, w_out_hbm, layer_scale_hbm, cotangent_hbm,
    block_hbm, grad_hbm, small_out, large_out,
    block_out, grad_field, store,
    field, taps, gain, w_in, b_in, w_out, layer_scale, cotangent, load,
    pad, d_pad, conv, hat, normed, d_branch, inv_all, tmp, d_hidden, slope, branch,
    rows_out, cols_out, rows_in, cols_in, corners_in,
    d_rows_out, d_cols_out, d_rows_in, d_cols_in, d_corners_in,
    part, part_in, x_out, x_in, y_out, y_in, z_out, z_in, zy_tmp, zy_out, zy_in, yz_out, yz_in,
    sums, sums_out, sums_in, sx, sy_a, sz_b, sz_a, sy_b,
    halo_send, halo_recv, d_halo_send, d_halo_recv,
    core_send, core_recv, x_send, x_recv, y_send, y_recv, z_send, z_recv,
    zy_send, zy_recv, yz_send, yz_recv,
    s_core_send, s_core_recv, sx_send, sx_recv, s3_send, s3_recv, s4_send, s4_recv,
):
    loads = [
        pltpu.make_async_copy(src, dst, load.at[at])
        for at, (src, dst) in enumerate((
            (field_hbm, field),
            (cotangent_hbm, cotangent),
            (layer_scale_hbm, layer_scale),
            (taps_hbm, taps),
            (gain_hbm, gain),
            (w_in_hbm, w_in),
            (b_in_hbm, b_in),
            (w_out_hbm, w_out),
        ))
    ]

    place = Place()
    core, x, y, z = place.core, place.x, place.y, place.z

    barrier = pltpu.get_barrier_semaphore()
    partners = [place.grid(*side) for side in SIDES[::-1]]
    partners += [place.on_x(lax.rem(x + k, N_X), c) for k in range(1, N_X) for c in range(2)]
    partners += [place.on_y(lax.rem(y + k, N_Y)) for k in range(1, N_Y)]
    partners += [place.on_z(lax.rem(z + k, N_Z)) for k in range(1, N_Z)]
    partners.append(place.sibling())
    for device in partners:
        pl.semaphore_signal(barrier, inc=1, device_id=device, device_id_type=MESH)
    for copy in loads:
        copy.start()

    loads[0].wait()
    for half in range(2):
        lanes = slice(half * HALF, (half + 1) * HALF)
        pad[half, 3 : 3 + ROWS, LEFT : LEFT + COLS, :] = field[:, :, lanes].astype(F32)
    halo_pack(pad, tmp, rows_out, cols_out)
    pl.semaphore_wait(barrier, len(partners))
    halos = halo_copies(place, rows_out, cols_out, rows_in, cols_in, corners_in, halo_send, halo_recv)
    for copy in halos[::-1]:
        copy.start()

    for copy in loads[1:]:
        copy.wait()
    wide_cot = cotangent[...].reshape(CELLS, CH).astype(F32)
    d_branch[...] = (layer_scale[...] * wide_cot).astype(BF16)
    for chunk in range(CHUNKS):
        d_hidden[chunk] = dot(d_branch[...], w_out[chunk * CHUNK : (chunk + 1) * CHUNK, :], 1, 1)
    z_out[...] = jnp.zeros_like(z_out)
    yz_out[...] = jnp.zeros_like(yz_out)
    sums[55:64, :] = jnp.zeros((9, CH), F32)

    for copy in halos:
        copy.wait()
    halo_unpack(place, pad, rows_in, cols_in, corners_in)

    depthwise(pad, taps, conv, False)
    parts = [conv[half].reshape(CELLS, HALF) for half in range(2)]
    mean = jnp.sum(parts[0] + parts[1], axis=-1, keepdims=True) * (1.0 / CH)
    parts = [value - mean for value in parts]
    spread = jnp.sum(parts[0] * parts[0] + parts[1] * parts[1], axis=-1, keepdims=True) * (1.0 / CH)
    inv_dev = lax.rsqrt(spread + LN_EPSILON)
    inv_all[...] = jnp.broadcast_to(inv_dev, (CELLS, HALF))
    for half in range(2):
        lanes = slice(half * HALF, (half + 1) * HALF)
        value = parts[half] * inv_dev
        hat[half] = value
        normed[:, lanes] = (value * gain[:, lanes]).astype(BF16)

    def send_on_core(which):
        copy = remote(
            part.at[which, :, :, 1 - core], part_in.at[which],
            core_send.at[which], core_recv.at[which], place.sibling(),
        )
        copy.start()
        return copy

    def send_on_x(which, core_copy):
        core_copy.wait()
        both = part[which, :, :, core].astype(F32) + part_in[which].astype(F32)
        x_out[which] = both.astype(BF16).reshape(2, N_X, 64, CH)
        copies = []
        for k in range(1, N_X):
            to = lax.rem(x + k, N_X)
            copy = remote(
                x_out.at[which, :, to], x_in.at[which, k - 1],
                x_send.at[which, k - 1], x_recv.at[which, k - 1], place.on_x(to),
            )
            copy.start()
            copies.append(copy)
        return copies

    total = jnp.zeros((CELLS, CH), F32)
    for chunk in range(CHUNKS):
        hidden_units = slice(chunk * CHUNK, (chunk + 1) * CHUNK)
        pre_act = dot(normed[...], w_in[:, hidden_units], 1, 0) + b_in[:, hidden_units]
        value, gelu_slope = gelu_pair(pre_act)
        hidden = value.astype(BF16)
        slope[chunk] = gelu_slope
        part[1, chunk] = dot(hidden, d_branch[...], 0, 0).astype(BF16).reshape(2, 2, 64, CH)
        total = total + dot(hidden, w_out[hidden_units, :], 1, 0)
    branch[...] = total
    core_out = send_on_core(1)

    d_normed = jnp.zeros((CELLS, CH), F32)
    for chunk in range(CHUNKS):
        hidden_units = slice(chunk * CHUNK, (chunk + 1) * CHUNK)
        d_pre = d_hidden[chunk] * slope[chunk]
        d_pre_b = d_pre.astype(BF16)
        part[0, chunk] = dot(d_pre_b, normed[...], 0, 0).astype(BF16).reshape(2, 2, 64, CH)
        d_normed = d_normed + dot(d_pre_b, w_in[:, hidden_units], 1, 1)
        sums[51 + chunk : 52 + chunk, :] = jnp.sum(d_pre, axis=0, keepdims=True)
    core_in = send_on_core(0)

    wide_cot = cotangent[...].reshape(CELLS, CH).astype(F32)
    sums[50:51, :] = jnp.sum(wide_cot * branch[...], axis=0, keepdims=True)

    hats = [hat[half] for half in range(2)]
    d_halves = [d_normed[:, half * HALF : (half + 1) * HALF] for half in range(2)]
    scaled = []
    for half in range(2):
        lanes = slice(half * HALF, (half + 1) * HALF)
        sums[49:50, lanes] = jnp.sum(d_halves[half] * hats[half], axis=0, keepdims=True)
        scaled.append(d_halves[half] * gain[:, lanes])
    m1 = jnp.sum(scaled[0] + scaled[1], axis=-1, keepdims=True) * (1.0 / CH)
    m2 = jnp.sum(scaled[0] * hats[0] + scaled[1] * hats[1], axis=-1, keepdims=True) * (1.0 / CH)
    for half in range(2):
        d_conv = inv_all[...] * (scaled[half] - m1 - hats[half] * m2)
        d_pad[half, 3 : 3 + ROWS, LEFT : LEFT + COLS, :] = d_conv.reshape(ROWS, COLS, HALF)


    x_copies_out = send_on_x(1, core_out)

    tap_sums(pad, d_pad, sums)

    def wait_slots(slots, send, recv, own, count, device_on):
        for k in range(1, count):
            other = lax.rem(own + k, count)
            remote(slots.at[own], slots.at[other], send.at[other], recv.at[other], device_on(other)).wait()

    def share(slots, send, recv, own, count, device_on):
        for k in range(1, count):
            other = lax.rem(own + k, count)
            remote(slots.at[own], slots.at[own], send.at[other], recv.at[own], device_on(other)).start()

    def gather_sum(slots, count):
        total = slots[0].astype(F32)
        for at in range(1, count):
            total = total + slots[at].astype(F32)
        return total

    sums_out[...] = sums[...].reshape(2, SUMS // 2, CH).astype(BF16)
    s_core = remote(sums_out.at[1 - core], sums_in, s_core_send, s_core_recv, place.sibling())
    s_core.start()
    halo_pack(d_pad, tmp, d_rows_out, d_cols_out)
    d_halos = halo_copies(
        place, d_rows_out, d_cols_out, d_rows_in, d_cols_in, d_corners_in, d_halo_send, d_halo_recv
    )
    for copy in d_halos:
        copy.start()

    x_copies_in = send_on_x(0, core_in)
    s_core.wait()
    total = (sums_out[core].astype(F32) + sums_in[...].astype(F32)).astype(BF16)
    sy_a[y] = total[0:16]
    sz_b[z] = total[16:32]
    share(sy_a, s3_send.at[0], s3_recv.at[0], y, N_Y, place.on_y)
    share(sz_b, s3_send.at[1], s3_recv.at[1], z, N_Z, place.on_z)

    block_out[...] = (
        field[...].reshape(CELLS, CH).astype(F32) + layer_scale[...] * branch[...]
    ).astype(BF16).reshape(ROWS, COLS, CH)
    block_store = pltpu.make_async_copy(block_out, block_hbm, store.at[0])
    block_store.start()

    def sum_on_x(which, copies):
        for copy in copies:
            copy.wait()
        total = x_out[which, :, x].astype(F32)
        for k in range(1, N_X):
            total = total + x_in[which, k - 1].astype(F32)
        return total

    def spread(into, send, recv, own, count, device_on, block):
        copies = []
        for k in range(1, count):
            to = lax.rem(own + k, count)
            copy = remote(block(to), into.at[k - 1], send.at[k - 1], recv.at[k - 1], device_on(to))
            copy.start()
            copies.append(copy)
        return copies

    def collect(copies, total, into):
        for copy in copies:
            copy.wait()
        for at in range(len(copies)):
            total = total + into[at].astype(F32)
        return total

    y_out[...] = sum_on_x(1, x_copies_out).astype(BF16).reshape(2, 4, 16, CH)
    y_copies = spread(
        y_in, y_send, y_recv, y, N_Y, place.on_y,
        lambda to: y_out.at[lax.rem(to, 2), to // 2],
    )
    total = sum_on_x(0, x_copies_in).reshape(2, 4, 16, CH)
    for on_y in range(N_Y):
        for on_z in range(N_Z):
            zy_tmp[on_z, 2 * on_y : 2 * on_y + 2, :] = total[on_y % 2, on_y // 2, 2 * on_z : 2 * on_z + 2]
    zy_out[...] = zy_tmp[...].astype(BF16)
    zy_copies = spread(
        zy_in, zy_send, zy_recv, z, N_Z, place.on_z, lambda to: zy_out.at[to]
    )

    wait_slots(sy_a, s3_send.at[0], s3_recv.at[0], y, N_Y, place.on_y)
    sz_a[z] = gather_sum(sy_a, N_Y).astype(BF16)
    share(sz_a, s4_send.at[0], s4_recv.at[0], z, N_Z, place.on_z)
    wait_slots(sz_b, s3_send.at[1], s3_recv.at[1], z, N_Z, place.on_z)
    sy_b[y] = gather_sum(sz_b, N_Z).astype(BF16)
    share(sy_b, s4_send.at[1], s4_recv.at[1], y, N_Y, place.on_y)

    for copy in d_halos:
        copy.wait()
    halo_unpack(place, d_pad, d_rows_in, d_cols_in, d_corners_in)
    depthwise(d_pad, taps, conv, True)
    for half in range(2):
        lanes = slice(half * HALF, (half + 1) * HALF)
        grad_field[:, :, lanes] = (cotangent[:, :, lanes].astype(F32) + conv[half]).astype(BF16)
    grad_store = pltpu.make_async_copy(grad_field, grad_hbm, store.at[1])
    grad_store.start()

    def pack(out, first, total):
        for to in range(8):
            for half in range(2):
                at = first + half * 2
                out[to, at : at + 2, :] = total[2 * to : 2 * to + 2, half * HALF : (half + 1) * HALF]

    pack(z_out, 4, collect(y_copies, y_out[place.y_lo, place.y_hi].astype(F32), y_in))
    z_copies = spread(z_in, z_send, z_recv, z, N_Z, place.on_z, lambda to: z_out.at[to])

    wait_slots(sz_a, s4_send.at[0], s4_recv.at[0], z, N_Z, place.on_z)
    wait_slots(sy_b, s4_send.at[1], s4_recv.at[1], y, N_Y, place.on_y)
    sx[core, x, 0:16] = gather_sum(sz_a, N_Z).astype(BF16)
    sx[core, x, 16:32] = gather_sum(sy_b, N_Y).astype(BF16)
    last = [(c, k) for c in range(2) for k in range(N_X) if (c, k) != (0, 0)]
    for c, k in last:
        c, k = lax.rem(core + c, 2), lax.rem(x + k, N_X)
        remote(
            sx.at[core, x], sx.at[core, x], sx_send.at[c, k], sx_recv.at[core, x], place.on_x(k, c)
        ).start()

    pack(yz_out, 0, collect(zy_copies, zy_out[z].astype(F32), zy_in))
    yz_copies = spread(yz_in, yz_send, yz_recv, y, N_Y, place.on_y, lambda to: yz_out.at[to])

    for c, k in last:
        c, k = lax.rem(core + c, 2), lax.rem(x + k, N_X)
        remote(
            sx.at[core, x], sx.at[c, k], sx_send.at[c, k], sx_recv.at[c, k], place.on_x(k, c)
        ).wait()
    for c in range(2):
        small_out[c * (SUMS // 2) : (c + 1) * (SUMS // 2), :] = gather_sum(sx.at[c], N_X) * FACTOR

    large_out[4:8, :] = collect(z_copies, z_out[z], z_in)[4:8] * FACTOR
    large_out[0:4, :] = collect(yz_copies, yz_out[y], yz_in)[0:4] * FACTOR
    block_store.wait()
    grad_store.wait()


def finish(
    block_in, grad_in_hbm, small_hbm, large_hbm,
    block_out, grad_field, grad_taps, grad_gain, grad_in, grad_bias, grad_out, grad_scale,
    small, large, move,
):
    moves = [
        pltpu.make_async_copy(src, dst, move.at[at])
        for at, (src, dst) in enumerate((
            (small_hbm, small), (large_hbm, large), (block_in, block_out), (grad_in_hbm, grad_field),
        ))
    ]
    for copy in moves:
        copy.start()
    moves[0].wait()
    moves[1].wait()
    for a in range(7):
        grad_taps[a] = small[a * 7 : a * 7 + 7, :]
    grad_gain[...] = small[49:50, :]
    grad_scale[...] = small[50:51, :]
    for chunk in range(CHUNKS):
        grad_bias[:, chunk * CHUNK : (chunk + 1) * CHUNK] = small[51 + chunk : 52 + chunk, :]
    for half in range(2):
        lanes = slice(half * HALF, (half + 1) * HALF)
        grad_in[:, lanes] = large[half * 2 : half * 2 + 2, :]
        grad_out[:, lanes] = large[4 + half * 2 : 6 + half * 2, :]
    moves[2].wait()
    moves[3].wait()


def local(field, kernel, gain, w_in, b_in, w_out, layer_scale, cotangent):
    vmem = pl.BlockSpec(memory_space=pltpu.VMEM)
    dma = pltpu.SemaphoreType.DMA
    halo = [
        pltpu.VMEM((2, 3, COLS, CH), BF16),
        pltpu.VMEM((2, 4 * ROWS, CH), BF16),
        pltpu.VMEM((2, 3, COLS, CH), BF16),
        pltpu.VMEM((2, 4 * ROWS, CH), BF16),
        pltpu.VMEM((4, 16, CH), BF16),
    ]
    hbm = pl.BlockSpec(memory_space=pltpu.HBM)
    scratch = [
        pltpu.VMEM((ROWS, COLS, CH), BF16),
        pltpu.VMEM((ROWS, COLS, CH), BF16),
        dma((2,)),
        pltpu.VMEM((ROWS, COLS, CH), BF16),
        pltpu.VMEM((7, 7, CH), F32),
        pltpu.VMEM((1, CH), F32),
        pltpu.VMEM((CH, FF), BF16),
        pltpu.VMEM((1, FF), F32),
        pltpu.VMEM((FF, CH), BF16),
        pltpu.VMEM((1, CH), F32),
        pltpu.VMEM((ROWS, COLS, CH), BF16),
        dma((8,)),
        pltpu.VMEM((2, ROWS + 6, COLS + 16, HALF), F32),
        pltpu.VMEM((2, ROWS + 6, COLS + 16, HALF), F32),
        pltpu.VMEM((2, ROWS, COLS, HALF), F32),
        pltpu.VMEM((2, CELLS, HALF), F32),
        pltpu.VMEM((CELLS, CH), BF16),
        pltpu.VMEM((CELLS, CH), BF16),
        pltpu.VMEM((CELLS, HALF), F32),
        pltpu.VMEM((2, 4 * ROWS, CH), F32),
        pltpu.VMEM((CHUNKS, CELLS, CHUNK), F32),
        pltpu.VMEM((CHUNKS, CELLS, CHUNK), F32),
        pltpu.VMEM((CELLS, CH), F32),
        *halo,
        *halo,
        pltpu.VMEM((2, CHUNKS, 2, 2, 64, CH), BF16),
        pltpu.VMEM((2, CHUNKS, 2, 64, CH), BF16),
        pltpu.VMEM((2, 2, N_X, 64, CH), BF16),
        pltpu.VMEM((2, N_X - 1, 2, 64, CH), BF16),
        pltpu.VMEM((2, 4, 16, CH), BF16),
        pltpu.VMEM((N_Y - 1, 16, CH), BF16),
        pltpu.VMEM((N_Z, 8, HALF), F32),
        pltpu.VMEM((N_Z - 1, 8, HALF), F32),
        pltpu.VMEM((N_Z, 16, CH), F32),
        pltpu.VMEM((N_Z, 16, CH), BF16),
        pltpu.VMEM((N_Z - 1, 16, CH), BF16),
        pltpu.VMEM((N_Y, 8, HALF), F32),
        pltpu.VMEM((N_Y - 1, 8, HALF), F32),
        pltpu.VMEM((SUMS, CH), F32),
        pltpu.VMEM((2, SUMS // 2, CH), BF16),
        pltpu.VMEM((SUMS // 2, CH), BF16),
        pltpu.VMEM((2, N_X, SUMS // 2, CH), BF16),
        pltpu.VMEM((N_Y, 16, CH), BF16),
        pltpu.VMEM((N_Z, 16, CH), BF16),
        pltpu.VMEM((N_Z, 16, CH), BF16),
        pltpu.VMEM((N_Y, 16, CH), BF16),
        dma((8,)), dma((8,)), dma((8,)), dma((8,)),
        dma((2,)), dma((2,)),
        dma((2, N_X - 1)), dma((2, N_X - 1)),
        dma((N_Y - 1,)), dma((N_Y - 1,)), dma((N_Z - 1,)), dma((N_Z - 1,)),
        dma((N_Z - 1,)), dma((N_Z - 1,)), dma((N_Y - 1,)), dma((N_Y - 1,)),
        dma, dma,
        dma((2, N_X)), dma((2, N_X)),
        dma((2, 8)), dma((2, 8)), dma((2, 8)), dma((2, 8)),
    ]
    grid_shape = jax.ShapeDtypeStruct(field.shape, BF16)
    mids = pl.pallas_call(
        step,
        out_shape=(
            grid_shape,
            grid_shape,
            jax.ShapeDtypeStruct((SUMS, CH), F32),
            jax.ShapeDtypeStruct((8, HALF), F32),
        ),
        in_specs=[hbm] * 8,
        out_specs=[hbm, hbm, vmem, vmem],
        scratch_shapes=scratch,
        compiler_params=pltpu.CompilerParams(
            collective_id=0, has_side_effects=True, vmem_limit_bytes=VMEM_GRANT
        ),
        name="block_step",
    )(
        field, kernel, gain.reshape(1, CH), w_in, b_in.reshape(1, FF), w_out,
        layer_scale.reshape(1, CH), cotangent,
    )
    block_out, grad_field, g_kernel, g_gain, g_in, g_bias, g_out, g_scale = pl.pallas_call(
        finish,
        out_shape=(
            grid_shape,
            grid_shape,
            jax.ShapeDtypeStruct((7, 7, CH), F32),
            jax.ShapeDtypeStruct((1, CH), F32),
            jax.ShapeDtypeStruct((2, CH), F32),
            jax.ShapeDtypeStruct((1, FF), F32),
            jax.ShapeDtypeStruct((2, CH), F32),
            jax.ShapeDtypeStruct((1, CH), F32),
        ),
        in_specs=[hbm] * 4,
        out_specs=[vmem] * 8,
        scratch_shapes=[pltpu.VMEM((SUMS, CH), F32), pltpu.VMEM((8, HALF), F32), dma((4,))],
        compiler_params=pltpu.CompilerParams(vmem_limit_bytes=VMEM_GRANT),
        name="write_outputs",
    )(*mids)
    return (
        block_out,
        grad_field,
        g_kernel,
        g_gain.reshape(CH),
        g_in.T,
        g_bias.reshape(FF),
        g_out,
        g_scale.reshape(CH),
    )


def solution(mesh):
    in_specs = (P("lat", "lon", None), P(), P(), P(), P(), P(), P(), P("lat", "lon", None))
    out_specs = (
        P("lat", "lon", None),
        P("lat", "lon", None),
        P(),
        P(),
        P(None, ("lat", "lon")),
        P(),
        P(("lat", "lon"), None),
        P(),
    )
    return jax.shard_map(local, mesh=mesh, in_specs=in_specs, out_specs=out_specs, check_vma=False)
```

```python
import jax
import jax.numpy as jnp
from jax import lax
from jax.experimental import pallas as pl
from jax.experimental.pallas import tpu as pltpu
from jax.sharding import PartitionSpec as P

GELU_K = 0.7978845608028654
GELU_C = 0.044715
LN_EPSILON = 1e-06
F32 = jnp.float32
BF16 = jnp.bfloat16
MESH = pl.DeviceIdType.MESH

N_X, N_Y, N_Z = 4, 8, 8
N_LAT, N_LON = 16, 32
ROWS, COLS, CH, FF = 8, 32, 256, 1024
CELLS = ROWS * COLS
HALF = 128
LEFT = 8
CHUNKS = 4
CHUNK = FF // CHUNKS
SUMS = 64
VMEM_GRANT = 62 * 2**20
FACTOR = 1.0 / 131072.0**0.5


def dot(left, right, over_left, over_right):
    return lax.dot_general(
        left, right, (((over_left,), (over_right,)), ((), ())), preferred_element_type=F32
    )


class Place:
    def __init__(self):
        self.lat = lax.axis_index("lat")
        self.lon = lax.axis_index("lon")
        self.core = lax.rem(self.lat, 2)
        self.x = lax.rem(self.lat // 2, N_X)
        self.y_lo = self.lat // 8
        self.z = lax.rem(self.lon, N_Z)
        self.y_hi = self.lon // N_Z
        self.y = self.y_hi * 2 + self.y_lo

    def grid(self, down, right):
        return (
            lax.rem(self.lat + down + N_LAT, N_LAT),
            lax.rem(self.lon + right + N_LON, N_LON),
        )

    def sibling(self):
        return (self.lat + 1 - 2 * self.core, self.lon)

    def on_x(self, x, core=None):
        return (self.y_lo * 8 + x * 2 + (self.core if core is None else core), self.lon)

    def on_y(self, y):
        return (lax.rem(y, 2) * 8 + self.x * 2 + self.core, (y // 2) * N_Z + self.z)

    def on_z(self, z):
        return (self.lat, self.y_hi * N_Z + z)


def remote(src, dst, send, recv, device):
    return pltpu.make_async_remote_copy(
        src_ref=src, dst_ref=dst, send_sem=send, recv_sem=recv, device_id=device, device_id_type=MESH
    )


SIDES = ((-1, 0), (1, 0), (0, -1), (0, 1), (-1, -1), (-1, 1), (1, -1), (1, 1))


def halo_pack(pad, tmp, rows_out, cols_out):
    for half in range(2):
        lanes = slice(half * HALF, (half + 1) * HALF)
        rows_out[0, :, :, lanes] = pad[half, 3:6, LEFT : LEFT + COLS, :].astype(BF16)
        rows_out[1, :, :, lanes] = pad[half, 8:11, LEFT : LEFT + COLS, :].astype(BF16)
        for row in range(ROWS):
            tmp[0, row * 4 : row * 4 + 4, lanes] = pad[half, 3 + row, LEFT : LEFT + 4, :]
            tmp[1, row * 4 : row * 4 + 4, lanes] = pad[half, 3 + row, LEFT + 28 : LEFT + 32, :]
    cols_out[...] = tmp[...].astype(BF16)


def halo_copies(place, rows_out, cols_out, rows_in, cols_in, corners_in, send, recv):
    pairs = (
        (rows_out.at[0], rows_in.at[1]),
        (rows_out.at[1], rows_in.at[0]),
        (cols_out.at[0], cols_in.at[1]),
        (cols_out.at[1], cols_in.at[0]),
        (cols_out.at[0, 0:16], corners_in.at[3]),
        (cols_out.at[1, 0:16], corners_in.at[2]),
        (cols_out.at[0, 16:32], corners_in.at[1]),
        (cols_out.at[1, 16:32], corners_in.at[0]),
    )
    return [
        remote(src, dst, send.at[at], recv.at[at], place.grid(*SIDES[at]))
        for at, (src, dst) in enumerate(pairs)
    ]


def halo_unpack(place, pad, rows_in, cols_in, corners_in):
    above = jnp.where(place.lat == 0, 0.0, 1.0).astype(F32)
    below = jnp.where(place.lat == N_LAT - 1, 0.0, 1.0).astype(F32)
    for half in range(2):
        lanes = slice(half * HALF, (half + 1) * HALF)
        pad[half, 0:3, LEFT : LEFT + COLS, :] = rows_in[0, :, :, lanes].astype(F32) * above
        pad[half, 11:14, LEFT : LEFT + COLS, :] = rows_in[1, :, :, lanes].astype(F32) * below
        for side, at in ((0, LEFT - 4), (1, LEFT + COLS)):
            wide = cols_in[side, :, lanes].astype(F32)
            for row in range(ROWS):
                pad[half, 3 + row, at : at + 4, :] = wide[row * 4 : row * 4 + 4]
            top = corners_in[side, :, lanes].astype(F32) * above
            bottom = corners_in[2 + side, :, lanes].astype(F32) * below
            for row in range(3):
                pad[half, row, at : at + 4, :] = top[4 + row * 4 : 8 + row * 4]
                pad[half, 11 + row, at : at + 4, :] = bottom[row * 4 : row * 4 + 4]


def depthwise(pad, taps, out, flipped):
    def one_half(half, carry):
        lanes = pl.ds(pl.multiple_of(half * HALF, HALF), HALF)
        for col in range(0, COLS, 8):
            summed = jnp.zeros((ROWS, 8, HALF), F32)
            for b in range(7):
                start = LEFT - 3 + b + col
                window = pad[half, :, start : start + 8, :]
                for a in range(7):
                    at = (6 - a, 6 - b) if flipped else (a, b)
                    tap = taps[at[0], at[1] : at[1] + 1, lanes]
                    summed = summed + window[a : a + ROWS] * tap[None]
            out[half, :, col : col + 8, :] = summed
        return carry

    lax.fori_loop(0, 2, one_half, 0)


def tap_sums(pad, d_pad, sums):
    def one_half(half, carry):
        lanes = pl.ds(pl.multiple_of(half * HALF, HALF), HALF)
        for b in range(7):
            totals = [jnp.zeros((8, HALF), F32) for _ in range(7)]
            for col in range(0, COLS, 8):
                start = LEFT - 3 + b + col
                window = pad[half, :, start : start + 8, :]
                grads = d_pad[half, 3 : 3 + ROWS, LEFT + col : LEFT + col + 8, :]
                for a in range(7):
                    totals[a] = totals[a] + jnp.sum(window[a : a + ROWS] * grads, axis=0)
            for a in range(7):
                at = a * 7 + b
                sums[at : at + 1, lanes] = jnp.sum(totals[a], axis=0, keepdims=True)
        return carry

    lax.fori_loop(0, 2, one_half, 0)


def gelu_pair(pre_act):
    square = pre_act * pre_act
    tanh_val = jnp.tanh(GELU_K * pre_act * (1.0 + GELU_C * square))
    half_up = 0.5 + 0.5 * tanh_val
    value = pre_act * half_up
    gelu_slope = half_up + value * (1.0 - tanh_val) * (GELU_K + (3.0 * GELU_C * GELU_K) * square)
    return value, gelu_slope


def step(
    field_hbm, taps_hbm, gain_hbm, w_in_hbm, b_in_hbm, w_out_hbm, layer_scale_hbm, cotangent_hbm,
    block_hbm, grad_hbm, small_out, large_out,
    block_out, grad_field, store,
    field, taps, gain, w_in, b_in, w_out, layer_scale, cotangent, load,
    pad, d_pad, conv, hat, normed, d_branch, inv_all, tmp, d_hidden, slope, branch,
    rows_out, cols_out, rows_in, cols_in, corners_in,
    d_rows_out, d_cols_out, d_rows_in, d_cols_in, d_corners_in,
    part, part_in, x_out, x_in, y_out, y_in, z_out, z_in, zy_tmp, zy_out, zy_in, yz_out, yz_in,
    sums, sums_out, sums_in, sx, sy_a, sz_b, sz_a, sy_b,
    halo_send, halo_recv, d_halo_send, d_halo_recv,
    core_send, core_recv, x_send, x_recv, y_send, y_recv, z_send, z_recv,
    zy_send, zy_recv, yz_send, yz_recv,
    s_core_send, s_core_recv, sx_send, sx_recv, s3_send, s3_recv, s4_send, s4_recv,
):
    loads = [
        pltpu.make_async_copy(src, dst, load.at[at])
        for at, (src, dst) in enumerate((
            (field_hbm, field),
            (cotangent_hbm, cotangent),
            (layer_scale_hbm, layer_scale),
            (taps_hbm, taps),
            (gain_hbm, gain),
            (w_in_hbm, w_in),
            (b_in_hbm, b_in),
            (w_out_hbm, w_out),
        ))
    ]

    place = Place()
    core, x, y, z = place.core, place.x, place.y, place.z

    barrier = pltpu.get_barrier_semaphore()
    partners = [place.grid(*side) for side in SIDES[::-1]]
    partners += [place.on_x(lax.rem(x + k, N_X), c) for k in range(1, N_X) for c in range(2)]
    partners += [place.on_y(lax.rem(y + k, N_Y)) for k in range(1, N_Y)]
    partners += [place.on_z(lax.rem(z + k, N_Z)) for k in range(1, N_Z)]
    partners.append(place.sibling())
    for device in partners:
        pl.semaphore_signal(barrier, inc=1, device_id=device, device_id_type=MESH)
    for copy in loads:
        copy.start()

    loads[0].wait()
    for half in range(2):
        lanes = slice(half * HALF, (half + 1) * HALF)
        pad[half, 3 : 3 + ROWS, LEFT : LEFT + COLS, :] = field[:, :, lanes].astype(F32)
    halo_pack(pad, tmp, rows_out, cols_out)
    pl.semaphore_wait(barrier, len(partners))
    halos = halo_copies(place, rows_out, cols_out, rows_in, cols_in, corners_in, halo_send, halo_recv)
    for copy in halos[::-1]:
        copy.start()

    for copy in loads[1:]:
        copy.wait()
    wide_cot = cotangent[...].reshape(CELLS, CH).astype(F32)
    d_branch[...] = (layer_scale[...] * wide_cot).astype(BF16)
    for chunk in range(CHUNKS):
        d_hidden[chunk] = dot(d_branch[...], w_out[chunk * CHUNK : (chunk + 1) * CHUNK, :], 1, 1)
    z_out[...] = jnp.zeros_like(z_out)
    yz_out[...] = jnp.zeros_like(yz_out)
    sums[55:64, :] = jnp.zeros((9, CH), F32)

    for copy in halos:
        copy.wait()
    halo_unpack(place, pad, rows_in, cols_in, corners_in)

    depthwise(pad, taps, conv, False)
    parts = [conv[half].reshape(CELLS, HALF) for half in range(2)]
    mean = jnp.sum(parts[0] + parts[1], axis=-1, keepdims=True) * (1.0 / CH)
    parts = [value - mean for value in parts]
    spread = jnp.sum(parts[0] * parts[0] + parts[1] * parts[1], axis=-1, keepdims=True) * (1.0 / CH)
    inv_dev = lax.rsqrt(spread + LN_EPSILON)
    inv_all[...] = jnp.broadcast_to(inv_dev, (CELLS, HALF))
    for half in range(2):
        lanes = slice(half * HALF, (half + 1) * HALF)
        value = parts[half] * inv_dev
        hat[half] = value
        normed[:, lanes] = (value * gain[:, lanes]).astype(BF16)

    def send_on_core(which):
        copy = remote(
            part.at[which, :, :, 1 - core], part_in.at[which],
            core_send.at[which], core_recv.at[which], place.sibling(),
        )
        copy.start()
        return copy

    def send_on_x(which, core_copy):
        core_copy.wait()
        both = part[which, :, :, core].astype(F32) + part_in[which].astype(F32)
        x_out[which] = both.astype(BF16).reshape(2, N_X, 64, CH)
        copies = []
        for k in range(1, N_X):
            to = lax.rem(x + k, N_X)
            copy = remote(
                x_out.at[which, :, to], x_in.at[which, k - 1],
                x_send.at[which, k - 1], x_recv.at[which, k - 1], place.on_x(to),
            )
            copy.start()
            copies.append(copy)
        return copies

    total = jnp.zeros((CELLS, CH), F32)
    for chunk in range(CHUNKS):
        hidden_units = slice(chunk * CHUNK, (chunk + 1) * CHUNK)
        pre_act = dot(normed[...], w_in[:, hidden_units], 1, 0) + b_in[:, hidden_units]
        value, gelu_slope = gelu_pair(pre_act)
        hidden = value.astype(BF16)
        slope[chunk] = gelu_slope
        part[1, chunk] = dot(hidden, d_branch[...], 0, 0).astype(BF16).reshape(2, 2, 64, CH)
        total = total + dot(hidden, w_out[hidden_units, :], 1, 0)
    branch[...] = total
    core_out = send_on_core(1)

    d_normed = jnp.zeros((CELLS, CH), F32)
    for chunk in range(CHUNKS):
        hidden_units = slice(chunk * CHUNK, (chunk + 1) * CHUNK)
        d_pre = d_hidden[chunk] * slope[chunk]
        d_pre_b = d_pre.astype(BF16)
        part[0, chunk] = dot(d_pre_b, normed[...], 0, 0).astype(BF16).reshape(2, 2, 64, CH)
        d_normed = d_normed + dot(d_pre_b, w_in[:, hidden_units], 1, 1)
        sums[51 + chunk : 52 + chunk, :] = jnp.sum(d_pre, axis=0, keepdims=True)
    core_in = send_on_core(0)

    wide_cot = cotangent[...].reshape(CELLS, CH).astype(F32)
    sums[50:51, :] = jnp.sum(wide_cot * branch[...], axis=0, keepdims=True)

    hats = [hat[half] for half in range(2)]
    d_halves = [d_normed[:, half * HALF : (half + 1) * HALF] for half in range(2)]
    scaled = []
    for half in range(2):
        lanes = slice(half * HALF, (half + 1) * HALF)
        sums[49:50, lanes] = jnp.sum(d_halves[half] * hats[half], axis=0, keepdims=True)
        scaled.append(d_halves[half] * gain[:, lanes])
    m1 = jnp.sum(scaled[0] + scaled[1], axis=-1, keepdims=True) * (1.0 / CH)
    m2 = jnp.sum(scaled[0] * hats[0] + scaled[1] * hats[1], axis=-1, keepdims=True) * (1.0 / CH)
    for half in range(2):
        d_conv = inv_all[...] * (scaled[half] - m1 - hats[half] * m2)
        d_pad[half, 3 : 3 + ROWS, LEFT : LEFT + COLS, :] = d_conv.reshape(ROWS, COLS, HALF)


    x_copies_out = send_on_x(1, core_out)

    tap_sums(pad, d_pad, sums)

    def wait_slots(slots, send, recv, own, count, device_on):
        for k in range(1, count):
            other = lax.rem(own + k, count)
            remote(slots.at[own], slots.at[other], send.at[other], recv.at[other], device_on(other)).wait()

    def share(slots, send, recv, own, count, device_on):
        for k in range(1, count):
            other = lax.rem(own + k, count)
            remote(slots.at[own], slots.at[own], send.at[other], recv.at[own], device_on(other)).start()

    def gather_sum(slots, count):
        total = slots[0].astype(F32)
        for at in range(1, count):
            total = total + slots[at].astype(F32)
        return total

    sums_out[...] = sums[...].reshape(2, SUMS // 2, CH).astype(BF16)
    s_core = remote(sums_out.at[1 - core], sums_in, s_core_send, s_core_recv, place.sibling())
    s_core.start()
    halo_pack(d_pad, tmp, d_rows_out, d_cols_out)
    d_halos = halo_copies(
        place, d_rows_out, d_cols_out, d_rows_in, d_cols_in, d_corners_in, d_halo_send, d_halo_recv
    )
    for copy in d_halos:
        copy.start()

    s_core.wait()
    total = (sums_out[core].astype(F32) + sums_in[...].astype(F32)).astype(BF16)
    sy_a[y] = total[0:16]
    sz_b[z] = total[16:32]
    share(sy_a, s3_send.at[0], s3_recv.at[0], y, N_Y, place.on_y)
    share(sz_b, s3_send.at[1], s3_recv.at[1], z, N_Z, place.on_z)
    x_copies_in = send_on_x(0, core_in)

    block_out[...] = (
        field[...].reshape(CELLS, CH).astype(F32) + layer_scale[...] * branch[...]
    ).astype(BF16).reshape(ROWS, COLS, CH)
    block_store = pltpu.make_async_copy(block_out, block_hbm, store.at[0])
    block_store.start()

    def sum_on_x(which, copies):
        for copy in copies:
            copy.wait()
        total = x_out[which, :, x].astype(F32)
        for k in range(1, N_X):
            total = total + x_in[which, k - 1].astype(F32)
        return total

    def spread(into, send, recv, own, count, device_on, block):
        copies = []
        for k in range(1, count):
            to = lax.rem(own + k, count)
            copy = remote(block(to), into.at[k - 1], send.at[k - 1], recv.at[k - 1], device_on(to))
            copy.start()
            copies.append(copy)
        return copies

    def collect(copies, total, into):
        for copy in copies:
            copy.wait()
        for at in range(len(copies)):
            total = total + into[at].astype(F32)
        return total

    y_out[...] = sum_on_x(1, x_copies_out).astype(BF16).reshape(2, 4, 16, CH)
    y_copies = spread(
        y_in, y_send, y_recv, y, N_Y, place.on_y,
        lambda to: y_out.at[lax.rem(to, 2), to // 2],
    )
    wait_slots(sy_a, s3_send.at[0], s3_recv.at[0], y, N_Y, place.on_y)
    sz_a[z] = gather_sum(sy_a, N_Y).astype(BF16)
    share(sz_a, s4_send.at[0], s4_recv.at[0], z, N_Z, place.on_z)
    wait_slots(sz_b, s3_send.at[1], s3_recv.at[1], z, N_Z, place.on_z)
    sy_b[y] = gather_sum(sz_b, N_Z).astype(BF16)
    share(sy_b, s4_send.at[1], s4_recv.at[1], y, N_Y, place.on_y)

    total = sum_on_x(0, x_copies_in).reshape(2, 4, 16, CH)
    for on_y in range(N_Y):
        for on_z in range(N_Z):
            zy_tmp[on_z, 2 * on_y : 2 * on_y + 2, :] = total[on_y % 2, on_y // 2, 2 * on_z : 2 * on_z + 2]
    zy_out[...] = zy_tmp[...].astype(BF16)
    zy_copies = spread(
        zy_in, zy_send, zy_recv, z, N_Z, place.on_z, lambda to: zy_out.at[to]
    )

    for copy in d_halos:
        copy.wait()
    halo_unpack(place, d_pad, d_rows_in, d_cols_in, d_corners_in)
    depthwise(d_pad, taps, conv, True)
    for half in range(2):
        lanes = slice(half * HALF, (half + 1) * HALF)
        grad_field[:, :, lanes] = (cotangent[:, :, lanes].astype(F32) + conv[half]).astype(BF16)
    grad_store = pltpu.make_async_copy(grad_field, grad_hbm, store.at[1])
    grad_store.start()

    def pack(out, first, total):
        for to in range(8):
            for half in range(2):
                at = first + half * 2
                out[to, at : at + 2, :] = total[2 * to : 2 * to + 2, half * HALF : (half + 1) * HALF]

    pack(z_out, 4, collect(y_copies, y_out[place.y_lo, place.y_hi].astype(F32), y_in))
    z_copies = spread(z_in, z_send, z_recv, z, N_Z, place.on_z, lambda to: z_out.at[to])

    wait_slots(sz_a, s4_send.at[0], s4_recv.at[0], z, N_Z, place.on_z)
    wait_slots(sy_b, s4_send.at[1], s4_recv.at[1], y, N_Y, place.on_y)
    sx[core, x, 0:16] = gather_sum(sz_a, N_Z).astype(BF16)
    sx[core, x, 16:32] = gather_sum(sy_b, N_Y).astype(BF16)
    last = [(c, k) for c in range(2) for k in range(N_X) if (c, k) != (0, 0)]
    for c, k in last:
        c, k = lax.rem(core + c, 2), lax.rem(x + k, N_X)
        remote(
            sx.at[core, x], sx.at[core, x], sx_send.at[c, k], sx_recv.at[core, x], place.on_x(k, c)
        ).start()

    pack(yz_out, 0, collect(zy_copies, zy_out[z].astype(F32), zy_in))
    yz_copies = spread(yz_in, yz_send, yz_recv, y, N_Y, place.on_y, lambda to: yz_out.at[to])

    for c, k in last:
        c, k = lax.rem(core + c, 2), lax.rem(x + k, N_X)
        remote(
            sx.at[core, x], sx.at[c, k], sx_send.at[c, k], sx_recv.at[c, k], place.on_x(k, c)
        ).wait()
    for c in range(2):
        small_out[c * (SUMS // 2) : (c + 1) * (SUMS // 2), :] = gather_sum(sx.at[c], N_X) * FACTOR

    large_out[4:8, :] = collect(z_copies, z_out[z], z_in)[4:8] * FACTOR
    large_out[0:4, :] = collect(yz_copies, yz_out[y], yz_in)[0:4] * FACTOR
    block_store.wait()
    grad_store.wait()


def finish(
    block_in, grad_in_hbm, small_hbm, large_hbm,
    block_out, grad_field, grad_taps, grad_gain, grad_in, grad_bias, grad_out, grad_scale,
    small, large, move,
):
    moves = [
        pltpu.make_async_copy(src, dst, move.at[at])
        for at, (src, dst) in enumerate((
            (small_hbm, small), (large_hbm, large), (block_in, block_out), (grad_in_hbm, grad_field),
        ))
    ]
    for copy in moves:
        copy.start()
    moves[0].wait()
    moves[1].wait()
    for a in range(7):
        grad_taps[a] = small[a * 7 : a * 7 + 7, :]
    grad_gain[...] = small[49:50, :]
    grad_scale[...] = small[50:51, :]
    for chunk in range(CHUNKS):
        grad_bias[:, chunk * CHUNK : (chunk + 1) * CHUNK] = small[51 + chunk : 52 + chunk, :]
    for half in range(2):
        lanes = slice(half * HALF, (half + 1) * HALF)
        grad_in[:, lanes] = large[half * 2 : half * 2 + 2, :]
        grad_out[:, lanes] = large[4 + half * 2 : 6 + half * 2, :]
    moves[2].wait()
    moves[3].wait()


def local(field, kernel, gain, w_in, b_in, w_out, layer_scale, cotangent):
    vmem = pl.BlockSpec(memory_space=pltpu.VMEM)
    dma = pltpu.SemaphoreType.DMA
    halo = [
        pltpu.VMEM((2, 3, COLS, CH), BF16),
        pltpu.VMEM((2, 4 * ROWS, CH), BF16),
        pltpu.VMEM((2, 3, COLS, CH), BF16),
        pltpu.VMEM((2, 4 * ROWS, CH), BF16),
        pltpu.VMEM((4, 16, CH), BF16),
    ]
    hbm = pl.BlockSpec(memory_space=pltpu.HBM)
    scratch = [
        pltpu.VMEM((ROWS, COLS, CH), BF16),
        pltpu.VMEM((ROWS, COLS, CH), BF16),
        dma((2,)),
        pltpu.VMEM((ROWS, COLS, CH), BF16),
        pltpu.VMEM((7, 7, CH), F32),
        pltpu.VMEM((1, CH), F32),
        pltpu.VMEM((CH, FF), BF16),
        pltpu.VMEM((1, FF), F32),
        pltpu.VMEM((FF, CH), BF16),
        pltpu.VMEM((1, CH), F32),
        pltpu.VMEM((ROWS, COLS, CH), BF16),
        dma((8,)),
        pltpu.VMEM((2, ROWS + 6, COLS + 16, HALF), F32),
        pltpu.VMEM((2, ROWS + 6, COLS + 16, HALF), F32),
        pltpu.VMEM((2, ROWS, COLS, HALF), F32),
        pltpu.VMEM((2, CELLS, HALF), F32),
        pltpu.VMEM((CELLS, CH), BF16),
        pltpu.VMEM((CELLS, CH), BF16),
        pltpu.VMEM((CELLS, HALF), F32),
        pltpu.VMEM((2, 4 * ROWS, CH), F32),
        pltpu.VMEM((CHUNKS, CELLS, CHUNK), F32),
        pltpu.VMEM((CHUNKS, CELLS, CHUNK), F32),
        pltpu.VMEM((CELLS, CH), F32),
        *halo,
        *halo,
        pltpu.VMEM((2, CHUNKS, 2, 2, 64, CH), BF16),
        pltpu.VMEM((2, CHUNKS, 2, 64, CH), BF16),
        pltpu.VMEM((2, 2, N_X, 64, CH), BF16),
        pltpu.VMEM((2, N_X - 1, 2, 64, CH), BF16),
        pltpu.VMEM((2, 4, 16, CH), BF16),
        pltpu.VMEM((N_Y - 1, 16, CH), BF16),
        pltpu.VMEM((N_Z, 8, HALF), F32),
        pltpu.VMEM((N_Z - 1, 8, HALF), F32),
        pltpu.VMEM((N_Z, 16, CH), F32),
        pltpu.VMEM((N_Z, 16, CH), BF16),
        pltpu.VMEM((N_Z - 1, 16, CH), BF16),
        pltpu.VMEM((N_Y, 8, HALF), F32),
        pltpu.VMEM((N_Y - 1, 8, HALF), F32),
        pltpu.VMEM((SUMS, CH), F32),
        pltpu.VMEM((2, SUMS // 2, CH), BF16),
        pltpu.VMEM((SUMS // 2, CH), BF16),
        pltpu.VMEM((2, N_X, SUMS // 2, CH), BF16),
        pltpu.VMEM((N_Y, 16, CH), BF16),
        pltpu.VMEM((N_Z, 16, CH), BF16),
        pltpu.VMEM((N_Z, 16, CH), BF16),
        pltpu.VMEM((N_Y, 16, CH), BF16),
        dma((8,)), dma((8,)), dma((8,)), dma((8,)),
        dma((2,)), dma((2,)),
        dma((2, N_X - 1)), dma((2, N_X - 1)),
        dma((N_Y - 1,)), dma((N_Y - 1,)), dma((N_Z - 1,)), dma((N_Z - 1,)),
        dma((N_Z - 1,)), dma((N_Z - 1,)), dma((N_Y - 1,)), dma((N_Y - 1,)),
        dma, dma,
        dma((2, N_X)), dma((2, N_X)),
        dma((2, 8)), dma((2, 8)), dma((2, 8)), dma((2, 8)),
    ]
    grid_shape = jax.ShapeDtypeStruct(field.shape, BF16)
    mids = pl.pallas_call(
        step,
        out_shape=(
            grid_shape,
            grid_shape,
            jax.ShapeDtypeStruct((SUMS, CH), F32),
            jax.ShapeDtypeStruct((8, HALF), F32),
        ),
        in_specs=[hbm] * 8,
        out_specs=[hbm, hbm, vmem, vmem],
        scratch_shapes=scratch,
        compiler_params=pltpu.CompilerParams(
            collective_id=0, has_side_effects=True, vmem_limit_bytes=VMEM_GRANT
        ),
        name="block_step",
    )(
        field, kernel, gain.reshape(1, CH), w_in, b_in.reshape(1, FF), w_out,
        layer_scale.reshape(1, CH), cotangent,
    )
    block_out, grad_field, g_kernel, g_gain, g_in, g_bias, g_out, g_scale = pl.pallas_call(
        finish,
        out_shape=(
            grid_shape,
            grid_shape,
            jax.ShapeDtypeStruct((7, 7, CH), F32),
            jax.ShapeDtypeStruct((1, CH), F32),
            jax.ShapeDtypeStruct((2, CH), F32),
            jax.ShapeDtypeStruct((1, FF), F32),
            jax.ShapeDtypeStruct((2, CH), F32),
            jax.ShapeDtypeStruct((1, CH), F32),
        ),
        in_specs=[hbm] * 4,
        out_specs=[vmem] * 8,
        scratch_shapes=[pltpu.VMEM((SUMS, CH), F32), pltpu.VMEM((8, HALF), F32), dma((4,))],
        compiler_params=pltpu.CompilerParams(vmem_limit_bytes=VMEM_GRANT),
        name="write_outputs",
    )(*mids)
    return (
        block_out,
        grad_field,
        g_kernel,
        g_gain.reshape(CH),
        g_in.T,
        g_bias.reshape(FF),
        g_out,
        g_scale.reshape(CH),
    )


def solution(mesh):
    in_specs = (P("lat", "lon", None), P(), P(), P(), P(), P(), P(), P("lat", "lon", None))
    out_specs = (
        P("lat", "lon", None),
        P("lat", "lon", None),
        P(),
        P(),
        P(None, ("lat", "lon")),
        P(),
        P(("lat", "lon"), None),
        P(),
    )
    return jax.shard_map(local, mesh=mesh, in_specs=in_specs, out_specs=out_specs, check_vma=False)
```

```python
import jax
import jax.numpy as jnp
from jax import lax
from jax.experimental import pallas as pl
from jax.experimental.pallas import tpu as pltpu
from jax.sharding import PartitionSpec as P

GELU_K = 0.7978845608028654
GELU_C = 0.044715
LN_EPSILON = 1e-06
F32 = jnp.float32
BF16 = jnp.bfloat16
MESH = pl.DeviceIdType.MESH

N_X, N_Y, N_Z = 4, 8, 8
N_LAT, N_LON = 16, 32
ROWS, COLS, CH, FF = 8, 32, 256, 1024
CELLS = ROWS * COLS
HALF = 128
LEFT = 8
CHUNKS = 4
CHUNK = FF // CHUNKS
SUMS = 64
VMEM_GRANT = 62 * 2**20
FACTOR = 1.0 / 131072.0**0.5


def dot(left, right, over_left, over_right):
    return lax.dot_general(
        left, right, (((over_left,), (over_right,)), ((), ())), preferred_element_type=F32
    )


class Place:
    def __init__(self):
        self.lat = lax.axis_index("lat")
        self.lon = lax.axis_index("lon")
        self.core = lax.rem(self.lat, 2)
        self.x = lax.rem(self.lat // 2, N_X)
        self.y_lo = self.lat // 8
        self.z = lax.rem(self.lon, N_Z)
        self.y_hi = self.lon // N_Z
        self.y = self.y_hi * 2 + self.y_lo

    def grid(self, down, right):
        return (
            lax.rem(self.lat + down + N_LAT, N_LAT),
            lax.rem(self.lon + right + N_LON, N_LON),
        )

    def sibling(self):
        return (self.lat + 1 - 2 * self.core, self.lon)

    def on_x(self, x, core=None):
        return (self.y_lo * 8 + x * 2 + (self.core if core is None else core), self.lon)

    def on_y(self, y):
        return (lax.rem(y, 2) * 8 + self.x * 2 + self.core, (y // 2) * N_Z + self.z)

    def on_z(self, z):
        return (self.lat, self.y_hi * N_Z + z)


def remote(src, dst, send, recv, device):
    return pltpu.make_async_remote_copy(
        src_ref=src, dst_ref=dst, send_sem=send, recv_sem=recv, device_id=device, device_id_type=MESH
    )


SIDES = ((-1, 0), (1, 0), (0, -1), (0, 1), (-1, -1), (-1, 1), (1, -1), (1, 1))


def halo_pack(pad, tmp, rows_out, cols_out):
    for half in range(2):
        lanes = slice(half * HALF, (half + 1) * HALF)
        rows_out[0, :, :, lanes] = pad[half, 3:6, LEFT : LEFT + COLS, :].astype(BF16)
        rows_out[1, :, :, lanes] = pad[half, 8:11, LEFT : LEFT + COLS, :].astype(BF16)
        for row in range(ROWS):
            tmp[0, row * 4 : row * 4 + 4, lanes] = pad[half, 3 + row, LEFT : LEFT + 4, :]
            tmp[1, row * 4 : row * 4 + 4, lanes] = pad[half, 3 + row, LEFT + 28 : LEFT + 32, :]
    cols_out[...] = tmp[...].astype(BF16)


def halo_copies(place, rows_out, cols_out, rows_in, cols_in, corners_in, send, recv):
    pairs = (
        (rows_out.at[0], rows_in.at[1]),
        (rows_out.at[1], rows_in.at[0]),
        (cols_out.at[0], cols_in.at[1]),
        (cols_out.at[1], cols_in.at[0]),
        (cols_out.at[0, 0:16], corners_in.at[3]),
        (cols_out.at[1, 0:16], corners_in.at[2]),
        (cols_out.at[0, 16:32], corners_in.at[1]),
        (cols_out.at[1, 16:32], corners_in.at[0]),
    )
    return [
        remote(src, dst, send.at[at], recv.at[at], place.grid(*SIDES[at]))
        for at, (src, dst) in enumerate(pairs)
    ]


def halo_unpack(place, pad, rows_in, cols_in, corners_in):
    above = jnp.where(place.lat == 0, 0.0, 1.0).astype(F32)
    below = jnp.where(place.lat == N_LAT - 1, 0.0, 1.0).astype(F32)
    for half in range(2):
        lanes = slice(half * HALF, (half + 1) * HALF)
        pad[half, 0:3, LEFT : LEFT + COLS, :] = rows_in[0, :, :, lanes].astype(F32) * above
        pad[half, 11:14, LEFT : LEFT + COLS, :] = rows_in[1, :, :, lanes].astype(F32) * below
        for side, at in ((0, LEFT - 4), (1, LEFT + COLS)):
            wide = cols_in[side, :, lanes].astype(F32)
            for row in range(ROWS):
                pad[half, 3 + row, at : at + 4, :] = wide[row * 4 : row * 4 + 4]
            top = corners_in[side, :, lanes].astype(F32) * above
            bottom = corners_in[2 + side, :, lanes].astype(F32) * below
            for row in range(3):
                pad[half, row, at : at + 4, :] = top[4 + row * 4 : 8 + row * 4]
                pad[half, 11 + row, at : at + 4, :] = bottom[row * 4 : row * 4 + 4]


def depthwise(pad, taps, out, flipped):
    def one_half(half, carry):
        lanes = pl.ds(pl.multiple_of(half * HALF, HALF), HALF)
        for col in range(0, COLS, 8):
            summed = jnp.zeros((ROWS, 8, HALF), F32)
            for b in range(7):
                start = LEFT - 3 + b + col
                window = pad[half, :, start : start + 8, :]
                for a in range(7):
                    at = (6 - a, 6 - b) if flipped else (a, b)
                    tap = taps[at[0], at[1] : at[1] + 1, lanes]
                    summed = summed + window[a : a + ROWS] * tap[None]
            out[half, :, col : col + 8, :] = summed
        return carry

    lax.fori_loop(0, 2, one_half, 0)


def tap_sums(pad, d_pad, sums):
    def one_half(half, carry):
        lanes = pl.ds(pl.multiple_of(half * HALF, HALF), HALF)
        for b in range(7):
            totals = [jnp.zeros((8, HALF), F32) for _ in range(7)]
            for col in range(0, COLS, 8):
                start = LEFT - 3 + b + col
                window = pad[half, :, start : start + 8, :]
                grads = d_pad[half, 3 : 3 + ROWS, LEFT + col : LEFT + col + 8, :]
                for a in range(7):
                    totals[a] = totals[a] + jnp.sum(window[a : a + ROWS] * grads, axis=0)
            for a in range(7):
                at = a * 7 + b
                sums[at : at + 1, lanes] = jnp.sum(totals[a], axis=0, keepdims=True)
        return carry

    lax.fori_loop(0, 2, one_half, 0)


def gelu_pair(pre_act):
    square = pre_act * pre_act
    tanh_val = jnp.tanh(GELU_K * pre_act * (1.0 + GELU_C * square))
    half_up = 0.5 + 0.5 * tanh_val
    value = pre_act * half_up
    gelu_slope = half_up + value * (1.0 - tanh_val) * (GELU_K + (3.0 * GELU_C * GELU_K) * square)
    return value, gelu_slope


def step(
    field_hbm, taps_hbm, gain_hbm, w_in_hbm, b_in_hbm, w_out_hbm, layer_scale_hbm, cotangent_hbm,
    block_hbm, grad_hbm, small_out, large_out,
    block_out, grad_field, store,
    field, taps, gain, w_in, b_in, w_out, layer_scale, cotangent, load,
    pad, d_pad, conv, hat, normed, d_branch, inv_all, tmp, d_hidden, slope, branch,
    rows_out, cols_out, rows_in, cols_in, corners_in,
    d_rows_out, d_cols_out, d_rows_in, d_cols_in, d_corners_in,
    part, part_in, x_out, x_in, y_out, y_in, z_out, z_in, zy_tmp, zy_out, zy_in, yz_out, yz_in,
    sums, sums_out, sums_in, sx, sy_a, sz_b, sz_a, sy_b,
    halo_send, halo_recv, d_halo_send, d_halo_recv,
    core_send, core_recv, x_send, x_recv, y_send, y_recv, z_send, z_recv,
    zy_send, zy_recv, yz_send, yz_recv,
    s_core_send, s_core_recv, sx_send, sx_recv, s3_send, s3_recv, s4_send, s4_recv,
):
    loads = [
        pltpu.make_async_copy(src, dst, load.at[at])
        for at, (src, dst) in enumerate((
            (field_hbm, field),
            (cotangent_hbm, cotangent),
            (layer_scale_hbm, layer_scale),
            (taps_hbm, taps),
            (gain_hbm, gain),
            (w_in_hbm, w_in),
            (b_in_hbm, b_in),
            (w_out_hbm, w_out),
        ))
    ]

    place = Place()
    core, x, y, z = place.core, place.x, place.y, place.z

    barrier = pltpu.get_barrier_semaphore()
    partners = [place.grid(*side) for side in SIDES[::-1]]
    partners += [place.on_x(lax.rem(x + k, N_X), c) for k in range(1, N_X) for c in range(2)]
    partners += [place.on_y(lax.rem(y + k, N_Y)) for k in range(1, N_Y)]
    partners += [place.on_z(lax.rem(z + k, N_Z)) for k in range(1, N_Z)]
    partners.append(place.sibling())
    for device in partners:
        pl.semaphore_signal(barrier, inc=1, device_id=device, device_id_type=MESH)
    for copy in loads:
        copy.start()

    loads[0].wait()
    for half in range(2):
        lanes = slice(half * HALF, (half + 1) * HALF)
        pad[half, 3 : 3 + ROWS, LEFT : LEFT + COLS, :] = field[:, :, lanes].astype(F32)
    halo_pack(pad, tmp, rows_out, cols_out)
    pl.semaphore_wait(barrier, len(partners))
    halos = halo_copies(place, rows_out, cols_out, rows_in, cols_in, corners_in, halo_send, halo_recv)
    for copy in halos[::-1]:
        copy.start()

    pending = []

    def arrived(copy):
        copy.wait_recv()
        pending.append(copy)

    for copy in loads[1:]:
        copy.wait()
    wide_cot = cotangent[...].reshape(CELLS, CH).astype(F32)
    d_branch[...] = (layer_scale[...] * wide_cot).astype(BF16)
    for chunk in range(CHUNKS):
        d_hidden[chunk] = dot(d_branch[...], w_out[chunk * CHUNK : (chunk + 1) * CHUNK, :], 1, 1)
    z_out[...] = jnp.zeros_like(z_out)
    yz_out[...] = jnp.zeros_like(yz_out)
    sums[55:64, :] = jnp.zeros((9, CH), F32)

    for copy in halos:
        arrived(copy)
    halo_unpack(place, pad, rows_in, cols_in, corners_in)

    depthwise(pad, taps, conv, False)
    parts = [conv[half].reshape(CELLS, HALF) for half in range(2)]
    mean = jnp.sum(parts[0] + parts[1], axis=-1, keepdims=True) * (1.0 / CH)
    parts = [value - mean for value in parts]
    spread = jnp.sum(parts[0] * parts[0] + parts[1] * parts[1], axis=-1, keepdims=True) * (1.0 / CH)
    inv_dev = lax.rsqrt(spread + LN_EPSILON)
    inv_all[...] = jnp.broadcast_to(inv_dev, (CELLS, HALF))
    for half in range(2):
        lanes = slice(half * HALF, (half + 1) * HALF)
        value = parts[half] * inv_dev
        hat[half] = value
        normed[:, lanes] = (value * gain[:, lanes]).astype(BF16)

    def send_on_core(which):
        copy = remote(
            part.at[which, :, :, 1 - core], part_in.at[which],
            core_send.at[which], core_recv.at[which], place.sibling(),
        )
        copy.start()
        return copy

    def send_on_x(which, core_copy):
        arrived(core_copy)
        both = part[which, :, :, core].astype(F32) + part_in[which].astype(F32)
        x_out[which] = both.astype(BF16).reshape(2, N_X, 64, CH)
        copies = []
        for k in range(1, N_X):
            to = lax.rem(x + k, N_X)
            copy = remote(
                x_out.at[which, :, to], x_in.at[which, k - 1],
                x_send.at[which, k - 1], x_recv.at[which, k - 1], place.on_x(to),
            )
            copy.start()
            copies.append(copy)
        return copies

    total = jnp.zeros((CELLS, CH), F32)
    for chunk in range(CHUNKS):
        hidden_units = slice(chunk * CHUNK, (chunk + 1) * CHUNK)
        pre_act = dot(normed[...], w_in[:, hidden_units], 1, 0) + b_in[:, hidden_units]
        value, gelu_slope = gelu_pair(pre_act)
        hidden = value.astype(BF16)
        slope[chunk] = gelu_slope
        part[1, chunk] = dot(hidden, d_branch[...], 0, 0).astype(BF16).reshape(2, 2, 64, CH)
        total = total + dot(hidden, w_out[hidden_units, :], 1, 0)
    branch[...] = total
    core_out = send_on_core(1)

    d_normed = jnp.zeros((CELLS, CH), F32)
    for chunk in range(CHUNKS):
        hidden_units = slice(chunk * CHUNK, (chunk + 1) * CHUNK)
        d_pre = d_hidden[chunk] * slope[chunk]
        d_pre_b = d_pre.astype(BF16)
        part[0, chunk] = dot(d_pre_b, normed[...], 0, 0).astype(BF16).reshape(2, 2, 64, CH)
        d_normed = d_normed + dot(d_pre_b, w_in[:, hidden_units], 1, 1)
        sums[51 + chunk : 52 + chunk, :] = jnp.sum(d_pre, axis=0, keepdims=True)
    core_in = send_on_core(0)

    wide_cot = cotangent[...].reshape(CELLS, CH).astype(F32)
    sums[50:51, :] = jnp.sum(wide_cot * branch[...], axis=0, keepdims=True)

    hats = [hat[half] for half in range(2)]
    d_halves = [d_normed[:, half * HALF : (half + 1) * HALF] for half in range(2)]
    scaled = []
    for half in range(2):
        lanes = slice(half * HALF, (half + 1) * HALF)
        sums[49:50, lanes] = jnp.sum(d_halves[half] * hats[half], axis=0, keepdims=True)
        scaled.append(d_halves[half] * gain[:, lanes])
    m1 = jnp.sum(scaled[0] + scaled[1], axis=-1, keepdims=True) * (1.0 / CH)
    m2 = jnp.sum(scaled[0] * hats[0] + scaled[1] * hats[1], axis=-1, keepdims=True) * (1.0 / CH)
    for half in range(2):
        d_conv = inv_all[...] * (scaled[half] - m1 - hats[half] * m2)
        d_pad[half, 3 : 3 + ROWS, LEFT : LEFT + COLS, :] = d_conv.reshape(ROWS, COLS, HALF)


    x_copies_out = send_on_x(1, core_out)

    tap_sums(pad, d_pad, sums)

    def wait_slots(slots, send, recv, own, count, device_on):
        for k in range(1, count):
            other = lax.rem(own + k, count)
            arrived(remote(slots.at[own], slots.at[other], send.at[other], recv.at[other], device_on(other)))

    def share(slots, send, recv, own, count, device_on):
        for k in range(1, count):
            other = lax.rem(own + k, count)
            remote(slots.at[own], slots.at[own], send.at[other], recv.at[own], device_on(other)).start()

    def gather_sum(slots, count):
        total = slots[0].astype(F32)
        for at in range(1, count):
            total = total + slots[at].astype(F32)
        return total

    sums_out[...] = sums[...].reshape(2, SUMS // 2, CH).astype(BF16)
    s_core = remote(sums_out.at[1 - core], sums_in, s_core_send, s_core_recv, place.sibling())
    s_core.start()
    halo_pack(d_pad, tmp, d_rows_out, d_cols_out)
    d_halos = halo_copies(
        place, d_rows_out, d_cols_out, d_rows_in, d_cols_in, d_corners_in, d_halo_send, d_halo_recv
    )
    for copy in d_halos:
        copy.start()

    arrived(s_core)
    total = (sums_out[core].astype(F32) + sums_in[...].astype(F32)).astype(BF16)
    sy_a[y] = total[0:16]
    sz_b[z] = total[16:32]
    share(sy_a, s3_send.at[0], s3_recv.at[0], y, N_Y, place.on_y)
    share(sz_b, s3_send.at[1], s3_recv.at[1], z, N_Z, place.on_z)
    x_copies_in = send_on_x(0, core_in)

    block_out[...] = (
        field[...].reshape(CELLS, CH).astype(F32) + layer_scale[...] * branch[...]
    ).astype(BF16).reshape(ROWS, COLS, CH)
    block_store = pltpu.make_async_copy(block_out, block_hbm, store.at[0])
    block_store.start()

    def sum_on_x(which, copies):
        for copy in copies:
            arrived(copy)
        total = x_out[which, :, x].astype(F32)
        for k in range(1, N_X):
            total = total + x_in[which, k - 1].astype(F32)
        return total

    def spread(into, send, recv, own, count, device_on, block):
        copies = []
        for k in range(1, count):
            to = lax.rem(own + k, count)
            copy = remote(block(to), into.at[k - 1], send.at[k - 1], recv.at[k - 1], device_on(to))
            copy.start()
            copies.append(copy)
        return copies

    def collect(copies, total, into):
        for copy in copies:
            arrived(copy)
        for at in range(len(copies)):
            total = total + into[at].astype(F32)
        return total

    y_out[...] = sum_on_x(1, x_copies_out).astype(BF16).reshape(2, 4, 16, CH)
    y_copies = spread(
        y_in, y_send, y_recv, y, N_Y, place.on_y,
        lambda to: y_out.at[lax.rem(to, 2), to // 2],
    )
    wait_slots(sy_a, s3_send.at[0], s3_recv.at[0], y, N_Y, place.on_y)
    sz_a[z] = gather_sum(sy_a, N_Y).astype(BF16)
    share(sz_a, s4_send.at[0], s4_recv.at[0], z, N_Z, place.on_z)
    wait_slots(sz_b, s3_send.at[1], s3_recv.at[1], z, N_Z, place.on_z)
    sy_b[y] = gather_sum(sz_b, N_Z).astype(BF16)
    share(sy_b, s4_send.at[1], s4_recv.at[1], y, N_Y, place.on_y)

    total = sum_on_x(0, x_copies_in).reshape(2, 4, 16, CH)
    for on_y in range(N_Y):
        for on_z in range(N_Z):
            zy_tmp[on_z, 2 * on_y : 2 * on_y + 2, :] = total[on_y % 2, on_y // 2, 2 * on_z : 2 * on_z + 2]
    zy_out[...] = zy_tmp[...].astype(BF16)
    zy_copies = spread(
        zy_in, zy_send, zy_recv, z, N_Z, place.on_z, lambda to: zy_out.at[to]
    )

    for copy in d_halos:
        arrived(copy)
    halo_unpack(place, d_pad, d_rows_in, d_cols_in, d_corners_in)
    depthwise(d_pad, taps, conv, True)
    for half in range(2):
        lanes = slice(half * HALF, (half + 1) * HALF)
        grad_field[:, :, lanes] = (cotangent[:, :, lanes].astype(F32) + conv[half]).astype(BF16)
    grad_store = pltpu.make_async_copy(grad_field, grad_hbm, store.at[1])
    grad_store.start()

    def pack(out, first, total):
        for to in range(8):
            for half in range(2):
                at = first + half * 2
                out[to, at : at + 2, :] = total[2 * to : 2 * to + 2, half * HALF : (half + 1) * HALF]

    pack(z_out, 4, collect(y_copies, y_out[place.y_lo, place.y_hi].astype(F32), y_in))
    z_copies = spread(z_in, z_send, z_recv, z, N_Z, place.on_z, lambda to: z_out.at[to])

    wait_slots(sz_a, s4_send.at[0], s4_recv.at[0], z, N_Z, place.on_z)
    wait_slots(sy_b, s4_send.at[1], s4_recv.at[1], y, N_Y, place.on_y)
    sx[core, x, 0:16] = gather_sum(sz_a, N_Z).astype(BF16)
    sx[core, x, 16:32] = gather_sum(sy_b, N_Y).astype(BF16)
    last = [(c, k) for c in range(2) for k in range(N_X) if (c, k) != (0, 0)]
    for c, k in last:
        c, k = lax.rem(core + c, 2), lax.rem(x + k, N_X)
        remote(
            sx.at[core, x], sx.at[core, x], sx_send.at[c, k], sx_recv.at[core, x], place.on_x(k, c)
        ).start()

    pack(yz_out, 0, collect(zy_copies, zy_out[z].astype(F32), zy_in))
    yz_copies = spread(yz_in, yz_send, yz_recv, y, N_Y, place.on_y, lambda to: yz_out.at[to])

    while pending:
        pending.pop().wait_send()

    for c, k in last:
        c, k = lax.rem(core + c, 2), lax.rem(x + k, N_X)
        arrived(
            remote(sx.at[core, x], sx.at[c, k], sx_send.at[c, k], sx_recv.at[c, k], place.on_x(k, c))
        )
    for c in range(2):
        small_out[c * (SUMS // 2) : (c + 1) * (SUMS // 2), :] = gather_sum(sx.at[c], N_X) * FACTOR

    large_out[4:8, :] = collect(z_copies, z_out[z], z_in)[4:8] * FACTOR
    large_out[0:4, :] = collect(yz_copies, yz_out[y], yz_in)[0:4] * FACTOR
    while pending:
        pending.pop().wait_send()
    block_store.wait()
    grad_store.wait()


def finish(
    block_in, grad_in_hbm, small_hbm, large_hbm,
    block_out, grad_field, grad_taps, grad_gain, grad_in, grad_bias, grad_out, grad_scale,
    small, large, move,
):
    moves = [
        pltpu.make_async_copy(src, dst, move.at[at])
        for at, (src, dst) in enumerate((
            (small_hbm, small), (large_hbm, large), (block_in, block_out), (grad_in_hbm, grad_field),
        ))
    ]
    for copy in moves:
        copy.start()
    moves[0].wait()
    moves[1].wait()
    for a in range(7):
        grad_taps[a] = small[a * 7 : a * 7 + 7, :]
    grad_gain[...] = small[49:50, :]
    grad_scale[...] = small[50:51, :]
    for chunk in range(CHUNKS):
        grad_bias[:, chunk * CHUNK : (chunk + 1) * CHUNK] = small[51 + chunk : 52 + chunk, :]
    for half in range(2):
        lanes = slice(half * HALF, (half + 1) * HALF)
        grad_in[:, lanes] = large[half * 2 : half * 2 + 2, :]
        grad_out[:, lanes] = large[4 + half * 2 : 6 + half * 2, :]
    moves[2].wait()
    moves[3].wait()


def local(field, kernel, gain, w_in, b_in, w_out, layer_scale, cotangent):
    vmem = pl.BlockSpec(memory_space=pltpu.VMEM)
    dma = pltpu.SemaphoreType.DMA
    halo = [
        pltpu.VMEM((2, 3, COLS, CH), BF16),
        pltpu.VMEM((2, 4 * ROWS, CH), BF16),
        pltpu.VMEM((2, 3, COLS, CH), BF16),
        pltpu.VMEM((2, 4 * ROWS, CH), BF16),
        pltpu.VMEM((4, 16, CH), BF16),
    ]
    hbm = pl.BlockSpec(memory_space=pltpu.HBM)
    scratch = [
        pltpu.VMEM((ROWS, COLS, CH), BF16),
        pltpu.VMEM((ROWS, COLS, CH), BF16),
        dma((2,)),
        pltpu.VMEM((ROWS, COLS, CH), BF16),
        pltpu.VMEM((7, 7, CH), F32),
        pltpu.VMEM((1, CH), F32),
        pltpu.VMEM((CH, FF), BF16),
        pltpu.VMEM((1, FF), F32),
        pltpu.VMEM((FF, CH), BF16),
        pltpu.VMEM((1, CH), F32),
        pltpu.VMEM((ROWS, COLS, CH), BF16),
        dma((8,)),
        pltpu.VMEM((2, ROWS + 6, COLS + 16, HALF), F32),
        pltpu.VMEM((2, ROWS + 6, COLS + 16, HALF), F32),
        pltpu.VMEM((2, ROWS, COLS, HALF), F32),
        pltpu.VMEM((2, CELLS, HALF), F32),
        pltpu.VMEM((CELLS, CH), BF16),
        pltpu.VMEM((CELLS, CH), BF16),
        pltpu.VMEM((CELLS, HALF), F32),
        pltpu.VMEM((2, 4 * ROWS, CH), F32),
        pltpu.VMEM((CHUNKS, CELLS, CHUNK), F32),
        pltpu.VMEM((CHUNKS, CELLS, CHUNK), F32),
        pltpu.VMEM((CELLS, CH), F32),
        *halo,
        *halo,
        pltpu.VMEM((2, CHUNKS, 2, 2, 64, CH), BF16),
        pltpu.VMEM((2, CHUNKS, 2, 64, CH), BF16),
        pltpu.VMEM((2, 2, N_X, 64, CH), BF16),
        pltpu.VMEM((2, N_X - 1, 2, 64, CH), BF16),
        pltpu.VMEM((2, 4, 16, CH), BF16),
        pltpu.VMEM((N_Y - 1, 16, CH), BF16),
        pltpu.VMEM((N_Z, 8, HALF), F32),
        pltpu.VMEM((N_Z - 1, 8, HALF), F32),
        pltpu.VMEM((N_Z, 16, CH), F32),
        pltpu.VMEM((N_Z, 16, CH), BF16),
        pltpu.VMEM((N_Z - 1, 16, CH), BF16),
        pltpu.VMEM((N_Y, 8, HALF), F32),
        pltpu.VMEM((N_Y - 1, 8, HALF), F32),
        pltpu.VMEM((SUMS, CH), F32),
        pltpu.VMEM((2, SUMS // 2, CH), BF16),
        pltpu.VMEM((SUMS // 2, CH), BF16),
        pltpu.VMEM((2, N_X, SUMS // 2, CH), BF16),
        pltpu.VMEM((N_Y, 16, CH), BF16),
        pltpu.VMEM((N_Z, 16, CH), BF16),
        pltpu.VMEM((N_Z, 16, CH), BF16),
        pltpu.VMEM((N_Y, 16, CH), BF16),
        dma((8,)), dma((8,)), dma((8,)), dma((8,)),
        dma((2,)), dma((2,)),
        dma((2, N_X - 1)), dma((2, N_X - 1)),
        dma((N_Y - 1,)), dma((N_Y - 1,)), dma((N_Z - 1,)), dma((N_Z - 1,)),
        dma((N_Z - 1,)), dma((N_Z - 1,)), dma((N_Y - 1,)), dma((N_Y - 1,)),
        dma, dma,
        dma((2, N_X)), dma((2, N_X)),
        dma((2, 8)), dma((2, 8)), dma((2, 8)), dma((2, 8)),
    ]
    grid_shape = jax.ShapeDtypeStruct(field.shape, BF16)
    mids = pl.pallas_call(
        step,
        out_shape=(
            grid_shape,
            grid_shape,
            jax.ShapeDtypeStruct((SUMS, CH), F32),
            jax.ShapeDtypeStruct((8, HALF), F32),
        ),
        in_specs=[hbm] * 8,
        out_specs=[hbm, hbm, vmem, vmem],
        scratch_shapes=scratch,
        compiler_params=pltpu.CompilerParams(
            collective_id=0, has_side_effects=True, vmem_limit_bytes=VMEM_GRANT
        ),
        name="block_step",
    )(
        field, kernel, gain.reshape(1, CH), w_in, b_in.reshape(1, FF), w_out,
        layer_scale.reshape(1, CH), cotangent,
    )
    block_out, grad_field, g_kernel, g_gain, g_in, g_bias, g_out, g_scale = pl.pallas_call(
        finish,
        out_shape=(
            grid_shape,
            grid_shape,
            jax.ShapeDtypeStruct((7, 7, CH), F32),
            jax.ShapeDtypeStruct((1, CH), F32),
            jax.ShapeDtypeStruct((2, CH), F32),
            jax.ShapeDtypeStruct((1, FF), F32),
            jax.ShapeDtypeStruct((2, CH), F32),
            jax.ShapeDtypeStruct((1, CH), F32),
        ),
        in_specs=[hbm] * 4,
        out_specs=[vmem] * 8,
        scratch_shapes=[pltpu.VMEM((SUMS, CH), F32), pltpu.VMEM((8, HALF), F32), dma((4,))],
        compiler_params=pltpu.CompilerParams(vmem_limit_bytes=VMEM_GRANT),
        name="write_outputs",
    )(*mids)
    return (
        block_out,
        grad_field,
        g_kernel,
        g_gain.reshape(CH),
        g_in.T,
        g_bias.reshape(FF),
        g_out,
        g_scale.reshape(CH),
    )


def solution(mesh):
    in_specs = (P("lat", "lon", None), P(), P(), P(), P(), P(), P(), P("lat", "lon", None))
    out_specs = (
        P("lat", "lon", None),
        P("lat", "lon", None),
        P(),
        P(),
        P(None, ("lat", "lon")),
        P(),
        P(("lat", "lon"), None),
        P(),
    )
    return jax.shard_map(local, mesh=mesh, in_specs=in_specs, out_specs=out_specs, check_vma=False)
```
